128 devices in a mesh: ctx: 8 (over y, core), vocab: 16 (over z, x).
Axes of the slice: x: 4, y: 4, z: 4, core: 2. Of those that a mesh axis runs over, the one named last changes fastest.
Arguments:
- queries: bfloat16 [4096, 4096], P('ctx', 'vocab')
- key_rows: bfloat16 [4096, 512], P('ctx')
- value_rows: bfloat16 [4096, 512], P('ctx'), may hold values from -6 to 6
- sink_logits: float32 [64], P('vocab'), may hold values from -6 to 6
- out_weight: bfloat16 [4096, 2880], P('vocab'), may hold values from -0.09375 to 0.09375
- out_bias: float32 [2880], replicated, may hold values from -3 to 3
- residual: bfloat16 [4096, 2880], P('ctx', 'vocab'), may hold values from -3 to 3
- norm_gain: float32 [2880], replicated, may hold values from 0.5 to 1.5
- policy_hidden: bfloat16 [4096, 2880], P('ctx', 'vocab'), may hold values from -6 to 6
- ref_head: bfloat16 [2880, 24576], P(None, 'vocab')
- policy_head: bfloat16 [2880, 24576], P(None, 'vocab')
- token_ids: int32 [4096], P('ctx'), may hold values from 0 to 24575
- advantages: float32 [4096], P('ctx'), may hold values from -8 to 8
- positions: int32 [4096], P('ctx'), may hold values from 0 to 511, as said below
Outputs:
- divergence: float32 [4096], P('ctx')
- hidden_grad: float32 [2880, 4096], P('vocab', 'ctx')
The draws below stay inside these ranges and needn't reach their ends.
Inputs may be any that keep to these rules, and one draw needn't show every extreme that they name: positions[0] is 0; every other entry is 0, where a document starts, or one more than the entry before it; no document is longer than 512 tokens, and one has exactly 512.
All inputs are finite; a program needn't handle non-finite values.
Results may differ from the reference program's by a relative error of at most 0.02.
Values may be sent and summed in bfloat16 or wider, within the bound.
A program may use at most 128 MiB of HBM per device.

```python
import math
import jax
import jax.numpy as jnp
import numpy as np
from jax import lax

D = 2880
HEADS = 64
KV_HEADS = 8
HEAD_DIM = 64
WINDOW = 128
ROWS_DEV = 512
TOKENS = 4096
VOCAB = 24576
N_CTX = 8


def key_field(key):
    return jax.random.normal(key, (TOKENS, KV_HEADS, HEAD_DIM), jnp.float32)


def draw_key_rows(key, part):
    shared = key_field(key)
    return shared.reshape(TOKENS, KV_HEADS * HEAD_DIM).astype(jnp.bfloat16)


def draw_queries(key, part):
    key = jax.random.fold_in(key, 2)
    first = jax.random.fold_in(key, 0)
    fresh = jax.random.normal(first, (TOKENS, HEADS, HEAD_DIM), jnp.float32)
    return fresh.reshape(TOKENS, HEADS * HEAD_DIM).astype(jnp.bfloat16)


def draw_ref_head(key, part):
    key = jax.random.fold_in(key, 3)
    first = jax.random.fold_in(key, 0)
    weights = jax.random.normal(first, (D, VOCAB), jnp.float32) * (3.0 / math.sqrt(D))
    return weights.astype(jnp.bfloat16)


def draw_policy_head(key, part):
    key = jax.random.fold_in(key, 4)
    first = jax.random.fold_in(key, 0)
    weights = jax.random.normal(first, (D, VOCAB), jnp.float32) * (3.0 / math.sqrt(D))
    return weights.astype(jnp.bfloat16)


def draw_positions(key, part):
    key = jax.random.fold_in(key, 5)
    index = jnp.arange(TOKENS, dtype=jnp.int32)
    half = ROWS_DEV // 2
    random_starts = jax.random.randint(key, (TOKENS,), 0, ROWS_DEV) == 0
    kept_whole = (index > half) & (index < half + ROWS_DEV)
    forced = (index == 0) | (index % ROWS_DEV == half)
    starts = random_starts & jnp.logical_not(kept_whole) | forced
    begun = lax.cummax(jnp.where(starts, index, 0), axis=0)
    return (index - begun).astype(jnp.int32)


def with_ends(array, stream_key, smallest, largest):
    dims = array.shape
    place = [jax.random.randint(jax.random.fold_in(stream_key, axis), (), 0, dims[axis]) for axis in range(len(dims))]
    array = array.at[tuple(place)].set(smallest)
    longest = dims.index(max(dims))
    place[longest] = (place[longest] + 1) % dims[longest]
    return array.at[tuple(place)].set(largest)


def shard_levels(rng, dims, cuts, least, largest):
    def one(axis_at, parts):
        heights = jax.random.uniform(jax.random.fold_in(jax.random.fold_in(rng, 6), axis_at), (parts,), jnp.float32, least / len(cuts), largest / len(cuts))
        return jnp.repeat(jnp.exp(heights), dims[axis_at] // parts).reshape((-1,) + (1,) * (len(dims) - axis_at - 1))

    level = one(*cuts[0])
    for cut in cuts[1:]:
        level = level * one(*cut)
    return level


def cumulative_ranks(count, lean):
    loads = [(1 << 20) // math.isqrt(standing ** lean) + 1 for standing in range(1, count + 1)]
    scale = 1 + sum(loads) // (1 << 30)
    return np.cumsum(np.array([max(1, weight // scale) for weight in loads]))


def ranked(own_key, dims, number_of, slope):
    grid = cumulative_ranks(number_of, slope)
    pick = jax.random.randint(jax.random.fold_in(own_key, 1), dims, 0, int(grid[number_of - 1]))
    standing = jnp.searchsorted(jnp.asarray(grid, jnp.int32), pick, side="right")
    return jax.random.permutation(jax.random.fold_in(own_key, 2), number_of)[standing].astype(jnp.int32)


def scatter_about(stream_key, shape, scale, most, cuts=(), held_as=jnp.bfloat16):
    gain = shard_levels(stream_key, shape, cuts, -0.22, 0.18) if cuts else 1.0
    drawn = jax.random.normal(stream_key, shape, jnp.float32) * scale * gain
    return jnp.minimum(jnp.maximum(drawn, -most), most).astype(held_as)


def setup_inputs(seed: int = 0) -> dict:
    key_list = jax.random.split(jax.random.key(seed), 15)
    queries = draw_queries(jax.random.fold_in(key_list[14], 71), 0)
    key_rows = draw_key_rows(jax.random.fold_in(key_list[14], 71), 0)
    value_rows = scatter_about(key_list[2], (TOKENS, KV_HEADS * HEAD_DIM), 1.0, 6.0, ((0, 8),))
    sink_logits = scatter_about(key_list[3], (HEADS,), 2.0, 6.0, ((0, 16),), jnp.float32)
    out_weight = scatter_about(key_list[4], (HEADS * HEAD_DIM, D), (HEADS * HEAD_DIM) ** -0.5, 0.09375, ((0, 16),))
    out_bias = scatter_about(key_list[5], (D,), 0.5, 3.0, (), jnp.float32)
    residual = scatter_about(key_list[6], (TOKENS, D), 0.5, 3.0, ((0, 8), (1, 16)))
    norm_gain = jnp.clip(1.0 + 0.1 * jax.random.normal(key_list[7], (D,), jnp.float32), 0.5, 1.5)
    policy_hidden = scatter_about(key_list[8], (TOKENS, D), 1.0, 6.0, ((0, 8), (1, 16)))
    ref_head = draw_ref_head(jax.random.fold_in(key_list[14], 71), 0)
    policy_head = draw_policy_head(jax.random.fold_in(key_list[14], 71), 0)
    token_ids = with_ends(ranked(key_list[11], (TOKENS,), VOCAB, 2), jax.random.fold_in(key_list[11], 3), 0, VOCAB - 1).astype(jnp.int32)
    advantages = scatter_about(key_list[12], (TOKENS,), 2.0, 8.0, ((0, 8),), jnp.float32)
    positions = draw_positions(jax.random.fold_in(key_list[14], 71), 0)
    return dict(queries=queries, key_rows=key_rows, value_rows=value_rows, sink_logits=sink_logits, out_weight=out_weight, out_bias=out_bias, residual=residual, norm_gain=norm_gain, policy_hidden=policy_hidden, ref_head=ref_head, policy_head=policy_head, token_ids=token_ids, advantages=advantages, positions=positions)


def attend(queries, key_rows, value_rows, sink_logits, positions):
    group = HEADS // KV_HEADS
    query_all = queries.reshape(TOKENS, HEADS, HEAD_DIM).astype(jnp.float32)
    key_all = jnp.repeat(key_rows.reshape(TOKENS, KV_HEADS, HEAD_DIM), group, axis=1).astype(jnp.float32)
    value_all = jnp.repeat(value_rows.reshape(TOKENS, KV_HEADS, HEAD_DIM), group, axis=1).astype(jnp.float32)
    front = jnp.zeros((WINDOW, HEADS, HEAD_DIM), jnp.float32)
    key_all = jnp.concatenate([front, key_all], axis=0)
    value_all = jnp.concatenate([front, value_all], axis=0)
    offsets = (jnp.arange(ROWS_DEV)[:, None] + WINDOW - jnp.arange(ROWS_DEV + WINDOW)[None, :]).astype(jnp.int32)

    def one_block(block_index):
        start = (block_index * ROWS_DEV).astype(jnp.int32)
        query_block = lax.dynamic_slice_in_dim(query_all, start, ROWS_DEV, 0)
        key_block = lax.dynamic_slice_in_dim(key_all, start, ROWS_DEV + WINDOW, 0)
        value_block = lax.dynamic_slice_in_dim(value_all, start, ROWS_DEV + WINDOW, 0)
        places = lax.dynamic_slice_in_dim(positions, start, ROWS_DEV, 0)
        scores = jnp.einsum('rhd,khd->hrk', query_block, key_block) * HEAD_DIM ** (-0.5)
        allowed = (offsets >= 0) & (offsets < WINDOW) & (places[:, None] >= offsets)
        scores = jnp.where(allowed[None], scores, -jnp.inf)
        peak = jnp.maximum(lax.optimization_barrier(jnp.max(scores, axis=2)), sink_logits[:, None])
        raised = jnp.exp(scores - peak[:, :, None])
        totals = lax.optimization_barrier(jnp.sum(raised, axis=2)) + jnp.exp(sink_logits[:, None] - peak)
        weights = (raised / totals[:, :, None]).astype(jnp.bfloat16)
        mixed = jnp.einsum('hrk,khd->rhd', weights.astype(jnp.float32), value_block)
        return mixed.reshape(ROWS_DEV, HEADS * HEAD_DIM).astype(jnp.bfloat16)
    blocks = lax.map(one_block, jnp.arange(N_CTX, dtype=jnp.int32))
    return blocks.reshape(TOKENS, HEADS * HEAD_DIM)

def reference(queries, key_rows, value_rows, sink_logits, out_weight, out_bias, residual, norm_gain, policy_hidden, ref_head, policy_head, token_ids, advantages, positions):
    attended = attend(queries, key_rows, value_rows, sink_logits, positions)
    projected = jnp.dot(attended, out_weight, preferred_element_type=jnp.float32) + out_bias
    ref_hidden = (residual.astype(jnp.float32) + projected).astype(jnp.bfloat16)
    hidden_wide = ref_hidden.astype(jnp.float32)
    spread = lax.optimization_barrier(jnp.mean(hidden_wide * hidden_wide, axis=1, keepdims=True))
    ref_normed = (hidden_wide * lax.rsqrt(spread + 1e-05) * norm_gain).astype(jnp.bfloat16)
    head_turned = policy_head.T

    def one_block(block_index):
        start = (block_index * ROWS_DEV).astype(jnp.int32)
        normed_block = lax.dynamic_slice_in_dim(ref_normed, start, ROWS_DEV, 0)
        policy_block = lax.dynamic_slice_in_dim(policy_hidden, start, ROWS_DEV, 0)
        chosen = lax.dynamic_slice_in_dim(token_ids, start, ROWS_DEV, 0)
        gains = lax.dynamic_slice_in_dim(advantages, start, ROWS_DEV, 0)
        ref_logits = jnp.dot(normed_block, ref_head, preferred_element_type=jnp.float32)
        policy_logits = jnp.dot(policy_block, policy_head, preferred_element_type=jnp.float32)
        log_ref = jax.nn.log_softmax(ref_logits, axis=1)
        log_policy = jax.nn.log_softmax(policy_logits, axis=1)
        prob = jnp.exp(log_policy)
        divergence = lax.optimization_barrier(jnp.sum(prob * (log_policy - log_ref), axis=1))
        onehot = (jnp.arange(VOCAB, dtype=jnp.int32)[None, :] == chosen[:, None]).astype(jnp.float32)
        logit_grad = prob * (log_policy - log_ref - divergence[:, None]) - gains[:, None] * (onehot - prob)
        logit_grad = logit_grad.astype(jnp.bfloat16)
        grad_block = jnp.dot(logit_grad, head_turned, preferred_element_type=jnp.float32)
        return (divergence, grad_block)
    divergences, grads = lax.map(one_block, jnp.arange(N_CTX, dtype=jnp.int32))
    divergence = divergences.reshape(TOKENS)
    hidden_grad = grads.reshape(TOKENS, D).T
    return (divergence, hidden_grad)
```

```python
import functools

import jax
import jax.numpy as jnp
from jax import lax
from jax.experimental import pallas as pl
from jax.experimental.pallas import tpu as pltpu
from jax.sharding import PartitionSpec as P

MESH = pl.DeviceIdType.MESH
BF = jnp.bfloat16
F32 = jnp.float32
HEAD_DIM = 64
WINDOW = 128
SIDE = 4
GROUP = SIDE * SIDE
HALVES = 2
NT = (((1,), (1,)), ((), ()))


class Pool:
    def __init__(self, send_sems, recv_sems):
        self.send_sems, self.recv_sems = send_sems, recv_sems
        self.copies = []

    def start(self, src, dst, device):
        at = len(self.copies)
        copy = pltpu.make_async_remote_copy(
            src_ref=src,
            dst_ref=dst,
            send_sem=self.send_sems.at[at],
            recv_sem=self.recv_sems.at[at],
            device_id=device,
            device_id_type=MESH,
        )
        copy.start()
        self.copies.append(copy)
        return copy


def add_into(dst, src):
    dst[...] = (dst[...].astype(F32) + src[...].astype(F32)).astype(BF)


class Gather:
    def __init__(self, pool, place, buf, half):
        self.pool, self.place, self.buf, self.half = pool, place, buf, half

    def piece(self, da, db):
        return self.buf.at[self.place.block(da, db)]

    def send(self, piece, da, db):
        return self.pool.start(piece, piece, self.place.device(da, db))

    def s0(self):
        own = self.piece(0, 0)
        self.ap, self.am = self.send(own, 1, 0), self.send(own, -1, 0)
        self.bp0, self.bm0 = self.send(own, 0, 1), self.send(own, 0, -1)

    def s1(self):
        self.ap.wait_recv()
        got = self.piece(-1, 0)
        if self.half == 0:
            self.a2 = self.send(got, 1, 0)
        self.bp1, self.bm1 = self.send(got, 0, 1), self.send(got, 0, -1)

    def s2(self):
        self.am.wait_recv()
        got = self.piece(1, 0)
        if self.half == 1:
            self.a2 = self.send(got, -1, 0)
        self.bp2, self.bm2 = self.send(got, 0, 1), self.send(got, 0, -1)

    def s3(self):
        self.a2.wait_recv()
        got = self.piece(2, 0)
        self.bp3, self.bm3 = self.send(got, 0, 1), self.send(got, 0, -1)

    def s4(self):
        self.bp0.wait_recv()
        self.f0 = self.send(self.piece(0, -1), 0, 1)

    def s5(self):
        self.bp1.wait_recv()
        self.f1 = self.send(self.piece(-1, -1), 0, 1)

    def s6(self):
        self.bm2.wait_recv()
        self.f2 = self.send(self.piece(1, 1), 0, -1)

    def s7(self):
        self.bm3.wait_recv()
        self.f3 = self.send(self.piece(2, 1), 0, -1)

    def s8(self):
        for copy in (self.bm0, self.bm1, self.bp2, self.bp3, self.f0, self.f1, self.f2, self.f3):
            copy.wait_recv()


class Scatter:
    def __init__(self, pool, place, x, tp, tm, fp, fm, y, ta, fap, fam, half):
        self.pool, self.place, self.half = pool, place, half
        self.x, self.tp, self.tm, self.fp, self.fm = x, tp, tm, fp, fm
        self.y, self.ta, self.fap, self.fam = y, ta, fap, fam

    def group(self, db, first, count):
        return self.x.at[pl.ds(SIDE * self.place.along_b(db) + first, count)]

    def far(self):
        to = self.place.device
        self.c_tp = self.pool.start(self.group(2, 0, 2), self.tp, to(0, 1))
        self.c_tm = self.pool.start(self.group(2, 2, 2), self.tm, to(0, -1))

    def near(self):
        to = self.place.device
        self.c_fp2 = self.pool.start(self.group(1, 2, 2), self.fp.at[pl.ds(2, 2)], to(0, 1))
        self.c_fm0 = self.pool.start(self.group(-1, 0, 2), self.fm.at[pl.ds(0, 2)], to(0, -1))

    def pass_on(self):
        to = self.place.device
        self.c_tp.wait_recv()
        add_into(self.group(1, 0, 2), self.tp)
        self.c_fp0 = self.pool.start(self.group(1, 0, 2), self.fp.at[pl.ds(0, 2)], to(0, 1))
        self.c_tm.wait_recv()
        add_into(self.group(-1, 2, 2), self.tm)
        self.c_fm2 = self.pool.start(self.group(-1, 2, 2), self.fm.at[pl.ds(2, 2)], to(0, -1))

    def turn(self):
        to = self.place.device
        for copy in (self.c_fp2, self.c_fm0, self.c_fp0, self.c_fm2):
            copy.wait_recv()
        for i in range(SIDE):
            at = SIDE * self.place.b + i
            self.y[i] = (
                self.x[at].astype(F32) + self.fp[i].astype(F32) + self.fm[i].astype(F32)
            ).astype(BF)
        step = 1 if self.half == 0 else -1
        self.c_ta = self.pool.start(self.y.at[self.place.along_a(2)], self.ta, to(step, 0))
        direct = self.y.at[self.place.along_a(-step)]
        if self.half == 0:
            self.c_fam = self.pool.start(direct, self.fam, to(-1, 0))
        else:
            self.c_fap = self.pool.start(direct, self.fap, to(1, 0))

    def last_hop(self):
        to = self.place.device
        self.c_ta.wait_recv()
        if self.half == 0:
            block = self.y.at[self.place.along_a(1)]
            add_into(block, self.ta)
            self.c_fap = self.pool.start(block, self.fap, to(1, 0))
        else:
            block = self.y.at[self.place.along_a(-1)]
            add_into(block, self.ta)
            self.c_fam = self.pool.start(block, self.fam, to(-1, 0))

    def result(self):
        self.c_fap.wait_recv()
        self.c_fam.wait_recv()
        return (
            self.y[self.place.a].astype(F32)
            + self.fap[...].astype(F32)
            + self.fam[...].astype(F32)
        )


class Place:
    def __init__(self):
        self.ctx, self.vocab = lax.axis_index("ctx"), lax.axis_index("vocab")
        self.z, self.x = self.vocab // SIDE, lax.rem(self.vocab, SIDE)
        self.core = lax.rem(self.ctx, 2)
        self.a = self.x * (1 - self.core) + self.z * self.core
        self.b = self.z * (1 - self.core) + self.x * self.core

    def along_a(self, da):
        return lax.rem(self.a + (da + SIDE), SIDE)

    def along_b(self, db):
        return lax.rem(self.b + (db + SIDE), SIDE)

    def block(self, da, db):
        return SIDE * self.along_b(db) + self.along_a(da)

    def device(self, da, db):
        a, b = self.along_a(da), self.along_b(db)
        return (self.ctx, a * (1 + 3 * self.core) + b * (4 - 3 * self.core))

    def block_of(self, vocab):
        turned = SIDE * lax.rem(vocab, SIDE) + vocab // SIDE
        return vocab * (1 - self.core) + turned * self.core


def column(row):
    return jnp.broadcast_to(row, (128, 128)).T


def kernel(
    queries,
    key_rows,
    value_rows,
    sinks,
    out_weight_hbm,
    bias,
    residual,
    gain,
    policy_hidden,
    ref_head_hbm,
    policy_head_hbm,
    token_ids,
    advantages,
    positions,
    divergence_out,
    grad_out,
    out_weight,
    ref_head,
    policy_head,
    head_blocks,
    kv,
    attended,
    land_policy,
    land_residual,
    residual_own,
    policy_rows,
    normed_rows,
    partial_rows,
    policy_logits,
    ref_logits,
    logit_grad,
    grad_parts,
    pol_max,
    pol_sum,
    stats,
    p_tp,
    p_tm,
    p_fp,
    p_fm,
    p_y,
    p_ta,
    p_fap,
    p_fam,
    g_tp,
    g_tm,
    g_fp,
    g_fm,
    g_y,
    g_ta,
    g_fap,
    g_fam,
    local_sems,
    send_sems,
    recv_sems,
    policy_sems,
    residual_sems,
    stat_sems,
):
    rows, width = attended.shape[0], out_weight.shape[1]
    half_rows = rows // HALVES
    piece = half_rows // GROUP
    share = land_policy.shape[3]
    vocab_here = ref_head.shape[1]
    place = Place()
    me = place.vocab
    own = place.block(0, 0)

    loads = [
        pltpu.make_async_copy(src, dst, local_sems.at[i])
        for i, (src, dst) in enumerate(
            (
                (out_weight_hbm, out_weight),
                (policy_head_hbm, policy_head),
                (ref_head_hbm, ref_head),
            )
        )
    ]
    for load in loads:
        load.start()

    barrier = pltpu.get_barrier_semaphore()
    ctx_count = lax.axis_size("ctx")
    next_ctx = lax.rem(place.ctx + 1, ctx_count)
    last_ctx = lax.rem(place.ctx + ctx_count - 1, ctx_count)
    for other in (next_ctx, last_ctx):
        pl.semaphore_signal(barrier, inc=1, device_id=(other, me), device_id_type=MESH)

    def greet(t, carry):
        pl.semaphore_signal(
            barrier,
            inc=1,
            device_id=(place.ctx, lax.rem(me + t, GROUP)),
            device_id_type=MESH,
        )
        return carry

    lax.fori_loop(1, GROUP, greet, 0)

    kv_lanes = pl.ds(pl.multiple_of(place.z * 128, 128), 128)
    upper = lax.rem(me // 2, 2) == 1
    for source, lane in ((key_rows, 0), (value_rows, HEAD_DIM)):
        pair = source[:, kv_lanes]
        kv[pl.ds(WINDOW, rows), lane : lane + HEAD_DIM] = jnp.where(
            upper, pair[:, HEAD_DIM:], pair[:, :HEAD_DIM]
        )
    own_rows = pl.ds(pl.multiple_of(own * piece, piece), piece)
    land_policy[me] = policy_hidden[:, own_rows, :]
    land_residual[me] = residual[:, own_rows, :]

    pl.semaphore_wait(barrier, GROUP - 1 + 2)

    pool = Pool(send_sems, recv_sems)
    halo = pool.start(kv.at[pl.ds(rows, WINDOW)], kv.at[pl.ds(0, WINDOW)], (next_ctx, me))

    def spread(source, land, sems, t):
        to = lax.rem(me + t, GROUP)
        block = pl.ds(pl.multiple_of(place.block_of(to) * piece, piece), piece)
        return pltpu.make_async_remote_copy(
            src_ref=source.at[:, block, :],
            dst_ref=land.at[me],
            send_sem=sems.at[0, t - 1],
            recv_sem=sems.at[1, t - 1],
            device_id=(place.ctx, to),
            device_id_type=MESH,
        )

    def each_peer(act):
        def body(t, carry):
            act(t)
            return carry

        lax.fori_loop(1, GROUP, body, 0)

    each_peer(lambda t: spread(policy_hidden, land_policy, policy_sems, t).start())
    each_peer(lambda t: spread(residual, land_residual, residual_sems, t).start())

    def attend(block):
        at = block * WINDOW
        keys = kv[at : at + 2 * WINDOW, :HEAD_DIM]
        values = kv[at : at + 2 * WINDOW, HEAD_DIM:]
        query = queries[at : at + WINDOW, :]
        heads = query.shape[1] // HEAD_DIM
        offsets = (
            lax.broadcasted_iota(jnp.int32, (WINDOW, 2 * WINDOW), 0)
            + WINDOW
            - lax.broadcasted_iota(jnp.int32, (WINDOW, 2 * WINDOW), 1)
        )
        where_at = column(positions[block : block + 1, :].astype(F32))
        where_at = jnp.concatenate([where_at, where_at], axis=1)
        allowed = (offsets >= 0) & (offsets < WINDOW) & (where_at >= offsets.astype(F32))
        mixed = []
        for h in range(heads):
            scores = (
                lax.dot_general(
                    query[:, h * HEAD_DIM : (h + 1) * HEAD_DIM],
                    keys,
                    NT,
                    preferred_element_type=F32,
                )
                * HEAD_DIM**-0.5
            )
            scores = jnp.where(allowed, scores, -jnp.inf)
            sink = sinks[h]
            peak = jnp.maximum(jnp.max(scores, axis=1, keepdims=True), sink)
            raised = jnp.exp(scores - peak)
            total = jnp.sum(raised, axis=1, keepdims=True) + jnp.exp(sink - peak)
            weights = (raised / total).astype(BF)
            mixed.append(jnp.dot(weights, values, preferred_element_type=F32).astype(BF))
        attended[at : at + WINDOW, :] = jnp.concatenate(mixed, axis=1)

    def project(half):
        rows_in = attended[half * half_rows : (half + 1) * half_rows, :]
        for start in range(0, width, 512):
            stop = min(start + 512, width)
            partial_rows[half, :, :, start:stop] = (
                jnp.dot(rows_in, out_weight[:, start:stop], preferred_element_type=F32)
                .astype(BF)
                .reshape(GROUP, piece, stop - start)
            )

    policy_ag = [Gather(pool, place, policy_rows.at[h], h) for h in range(HALVES)]
    normed_ag = [Gather(pool, place, normed_rows.at[h], h) for h in range(HALVES)]

    def scatter(x, bufs, h):
        return Scatter(pool, place, x.at[h], *(buf.at[h] for buf in bufs), h)

    p_bufs = (p_tp, p_tm, p_fp, p_fm, p_y, p_ta, p_fap, p_fam)
    g_bufs = (g_tp, g_tm, g_fp, g_fm, g_y, g_ta, g_fap, g_fam)
    partial_rs = [scatter(partial_rows, p_bufs, h) for h in range(HALVES)]
    grad_rs = [scatter(grad_parts, g_bufs, h) for h in range(HALVES)]

    def join(land, h):
        return jnp.concatenate([land[v, h] for v in range(GROUP)], axis=1)

    def normalise(h):
        projected = partial_rs[h].result() + bias[...]
        hidden = (residual_own[h].astype(F32) + projected).astype(BF)
        wide = hidden.astype(F32)
        spread_of = jnp.sum(wide * wide, axis=1, keepdims=True) * (1.0 / width)
        normed_rows[h, own] = (wide * lax.rsqrt(spread_of + 1e-05) * gain[...]).astype(BF)

    def logits(rows_of, head, out, h, tile, tiles=3):
        cols = slice(tile * (vocab_here // tiles), (tile + 1) * (vocab_here // tiles))
        lhs = rows_of[h].reshape(half_rows, width)
        out[h, :, cols] = jnp.dot(lhs, head[:, cols], preferred_element_type=F32)

    def policy_stats(h):
        top = jnp.max(policy_logits[h], axis=1, keepdims=True)
        pol_max[h] = jnp.broadcast_to(top, pol_max.shape[1:])
        pol_sum[h] = jnp.broadcast_to(
            jnp.sum(jnp.exp(policy_logits[h] - top), axis=1, keepdims=True), pol_sum.shape[1:]
        )

    def stat_copy(h, t):
        to = lax.rem(me + t, GROUP)
        return pltpu.make_async_remote_copy(
            src_ref=stats.at[h, me],
            dst_ref=stats.at[h, me],
            send_sem=stat_sems.at[h, 0, t - 1],
            recv_sem=stat_sems.at[h, 1, t - 1],
            device_id=(place.ctx, to),
            device_id_type=MESH,
        )

    def send_stats(h):
        top = jnp.max(ref_logits[h], axis=1, keepdims=True)
        total = jnp.sum(jnp.exp(ref_logits[h] - top), axis=1, keepdims=True)
        pol_top = pol_max[h][:, :1]
        gap = jnp.sum(
            jnp.exp(policy_logits[h] - pol_top) * (policy_logits[h] - ref_logits[h]),
            axis=1,
            keepdims=True,
        )
        lane = lax.broadcasted_iota(jnp.int32, (half_rows, 128), 1)
        packed = jnp.where(lane == 0, pol_max[h], pol_sum[h])
        packed = jnp.where(lane == 2, top, packed)
        packed = jnp.where(lane == 3, total, packed)
        packed = jnp.where(lane == 4, gap, packed)
        stats[h, me] = packed.T[:8, :]
        each_peer(lambda t: stat_copy(h, t).start())

    def loss_gradient(h):
        each_peer(lambda t: stat_copy(h, t).wait_recv())
        pol_tops, pol_sums = stats[h, :, 0, :], stats[h, :, 1, :]
        ref_tops, ref_sums = stats[h, :, 2, :], stats[h, :, 3, :]
        pol_top = jnp.max(pol_tops, axis=0, keepdims=True)
        ref_top = jnp.max(ref_tops, axis=0, keepdims=True)
        scale = jnp.exp(pol_tops - pol_top)
        pol_total = jnp.sum(pol_sums * scale, axis=0, keepdims=True)
        gap = jnp.sum(stats[h, :, 4, :] * scale, axis=0, keepdims=True) / pol_total
        ref_total = jnp.sum(ref_sums * jnp.exp(ref_tops - ref_top), axis=0, keepdims=True)
        log_pol = pol_top + jnp.log(pol_total)
        log_ref = ref_top + jnp.log(ref_total)
        divergence_out[h : h + 1, :] = gap - log_pol + log_ref
        for part in range(half_rows // 128):
            lanes = slice(part * 128, (part + 1) * 128)
            at = h * (half_rows // 128) + part
            here = slice(part * 128, (part + 1) * 128)
            adv_row = advantages[at : at + 1, :]
            log_col = column(log_pol[:, lanes])
            add_col = column(adv_row - gap[:, lanes])
            adv_col = column(adv_row)
            tok_col = column(
                (token_ids[at : at + 1, :] - me * vocab_here).astype(F32)
            )
            for chunk in range(0, vocab_here, 128):
                cols = slice(chunk, chunk + 128)
                ids = (lax.broadcasted_iota(jnp.int32, (128, 128), 1) + chunk).astype(F32)
                pol = policy_logits[h, here, cols]
                prob = jnp.exp(pol - log_col)
                value = prob * (pol - ref_logits[h, here, cols] + add_col)
                logit_grad[h, here, cols] = (
                    value - jnp.where(ids == tok_col, adv_col, 0.0)
                ).astype(BF)

    def gradient(h, db):
        at = pl.ds(SIDE * place.along_b(db), SIDE)
        block_rows = head_blocks.shape[1]
        lhs = head_blocks[at].reshape(SIDE * block_rows, vocab_here)
        grad_parts[h, at] = (
            lax.dot_general(lhs, logit_grad[h], NT, preferred_element_type=F32)
            .astype(BF)
            .reshape(SIDE, block_rows, half_rows)
        )

    def finish(h):
        grad_out[:, h * half_rows : (h + 1) * half_rows] = grad_rs[h].result()[:share, :]

    attend(1)
    halo.wait_recv()
    attend(0)
    each_peer(lambda t: spread(policy_hidden, land_policy, policy_sems, t).wait_recv())
    for h in range(HALVES):
        policy_rows[h, own] = join(land_policy, h)
        policy_ag[h].s0()
    loads[0].wait()
    project(0)
    partial_rs[0].far()
    partial_rs[0].near()
    attend(2)
    attend(3)
    project(1)
    partial_rs[1].far()
    partial_rs[1].near()
    for h in range(HALVES):
        policy_ag[h].s1()
        policy_ag[h].s2()
    for h in range(HALVES):
        partial_rs[h].pass_on()
    for h in range(HALVES):
        policy_ag[h].s4()
        policy_ag[h].s3()
    each_peer(lambda t: spread(residual, land_residual, residual_sems, t).wait_recv())
    for h in range(HALVES):
        residual_own[h] = join(land_residual, h)
    loads[1].wait()
    for d in range(GROUP):
        head_blocks[place.block_of(d), :share, :] = policy_head[d * share : (d + 1) * share, :]
    partial_rs[0].turn()
    partial_rs[1].turn()
    policy_ag[0].s5()
    policy_ag[0].s6()
    partial_rs[0].last_hop()
    partial_rs[1].last_hop()
    policy_ag[0].s7()
    normalise(0)
    normed_ag[0].s0()
    normalise(1)
    normed_ag[1].s0()
    policy_ag[1].s5()
    policy_ag[1].s6()
    policy_ag[1].s7()
    normed_ag[0].s1()
    normed_ag[0].s2()
    normed_ag[1].s1()
    normed_ag[1].s2()
    policy_ag[0].s8()
    logits(policy_rows, policy_head, policy_logits, 0, 0)
    normed_ag[0].s4()
    normed_ag[0].s3()
    logits(policy_rows, policy_head, policy_logits, 0, 1)
    normed_ag[1].s4()
    normed_ag[1].s3()
    normed_ag[0].s5()
    normed_ag[0].s6()
    logits(policy_rows, policy_head, policy_logits, 0, 2)
    normed_ag[0].s7()
    policy_ag[1].s8()
    logits(policy_rows, policy_head, policy_logits, 1, 0)
    normed_ag[1].s5()
    normed_ag[1].s6()
    logits(policy_rows, policy_head, policy_logits, 1, 1)
    normed_ag[1].s7()
    logits(policy_rows, policy_head, policy_logits, 1, 2)
    policy_stats(0)
    policy_stats(1)
    loads[2].wait()
    normed_ag[0].s8()
    for tile in range(3):
        logits(normed_rows, ref_head, ref_logits, 0, tile)
    send_stats(0)
    normed_ag[1].s8()
    logits(normed_rows, ref_head, ref_logits, 1, 0)
    logits(normed_rows, ref_head, ref_logits, 1, 1)
    loss_gradient(0)
    gradient(0, 2)
    grad_rs[0].far()
    gradient(0, 1)
    gradient(0, -1)
    grad_rs[0].near()
    gradient(0, 0)
    logits(normed_rows, ref_head, ref_logits, 1, 2)
    send_stats(1)
    grad_rs[0].pass_on()
    loss_gradient(1)
    gradient(1, 2)
    grad_rs[1].far()
    gradient(1, 1)
    gradient(1, -1)
    grad_rs[1].near()
    grad_rs[0].turn()
    gradient(1, 0)
    grad_rs[0].last_hop()
    grad_rs[1].pass_on()
    finish(0)
    grad_rs[1].turn()
    grad_rs[1].last_hop()
    finish(1)

    for copy in pool.copies:
        copy.wait_send()
    each_peer(lambda t: spread(policy_hidden, land_policy, policy_sems, t).wait_send())
    each_peer(lambda t: spread(residual, land_residual, residual_sems, t).wait_send())
    for h in range(HALVES):
        each_peer(lambda t: stat_copy(h, t).wait_send())


def shards(
    queries,
    key_rows,
    value_rows,
    sink_logits,
    out_weight,
    out_bias,
    residual,
    norm_gain,
    policy_hidden,
    ref_head,
    policy_head,
    token_ids,
    advantages,
    positions,
):
    rows, heads_width = queries.shape
    share = residual.shape[1]
    width, vocab_here = ref_head.shape
    half_rows = rows // HALVES
    piece = half_rows // GROUP
    block_rows = -(-share // 16) * 16
    copies = 1 + HALVES * (15 + 15 + 9 + 9)

    def sums(block):
        return [
            pltpu.VMEM((HALVES, *lead, *block), BF)
            for lead in ((2,), (2,), (SIDE,), (SIDE,), (SIDE,), (), (), ())
        ]

    vmem, hbm = (pl.BlockSpec(memory_space=space) for space in (pltpu.VMEM, pl.ANY))
    smem = pl.BlockSpec(memory_space=pltpu.SMEM)
    divergence, grad = pl.pallas_call(
        kernel,
        out_shape=(
            jax.ShapeDtypeStruct((HALVES, half_rows), F32),
            jax.ShapeDtypeStruct((share, rows), F32),
        ),
        in_specs=[
            vmem, vmem, vmem, smem, hbm, vmem, vmem, vmem, vmem, hbm, hbm, vmem, vmem, vmem,
        ],
        out_specs=(vmem, vmem),
        scratch_shapes=[
            pltpu.VMEM((heads_width, width), BF),
            pltpu.VMEM((width, vocab_here), BF),
            pltpu.VMEM((width, vocab_here), BF),
            pltpu.VMEM((GROUP, block_rows, vocab_here), BF),
            pltpu.VMEM((WINDOW + rows, 2 * HEAD_DIM), BF),
            pltpu.VMEM((rows, heads_width), BF),
            pltpu.VMEM((GROUP, HALVES, piece, share), BF),
            pltpu.VMEM((GROUP, HALVES, piece, share), BF),
            pltpu.VMEM((HALVES, piece, width), BF),
            pltpu.VMEM((HALVES, GROUP, piece, width), BF),
            pltpu.VMEM((HALVES, GROUP, piece, width), BF),
            pltpu.VMEM((HALVES, GROUP, piece, width), BF),
            pltpu.VMEM((HALVES, half_rows, vocab_here), F32),
            pltpu.VMEM((HALVES, half_rows, vocab_here), F32),
            pltpu.VMEM((HALVES, half_rows, vocab_here), BF),
            pltpu.VMEM((HALVES, GROUP, block_rows, half_rows), BF),
            pltpu.VMEM((HALVES, half_rows, 128), F32),
            pltpu.VMEM((HALVES, half_rows, 128), F32),
            pltpu.VMEM((HALVES, GROUP, 8, half_rows), F32),
            *sums((piece, width)),
            *sums((block_rows, half_rows)),
            pltpu.SemaphoreType.DMA((3,)),
            pltpu.SemaphoreType.DMA((copies,)),
            pltpu.SemaphoreType.DMA((copies,)),
            pltpu.SemaphoreType.DMA((2, GROUP - 1)),
            pltpu.SemaphoreType.DMA((2, GROUP - 1)),
            pltpu.SemaphoreType.DMA((HALVES, 2, GROUP - 1)),
        ],
        compiler_params=pltpu.CompilerParams(
            collective_id=0, has_side_effects=True, vmem_limit_bytes=62 << 20
        ),
    )(
        queries,
        key_rows,
        value_rows,
        sink_logits,
        out_weight,
        out_bias.reshape(1, width),
        residual.reshape(HALVES, half_rows, share),
        norm_gain.reshape(1, width),
        policy_hidden.reshape(HALVES, half_rows, share),
        ref_head,
        policy_head,
        token_ids.reshape(rows // 128, 128),
        advantages.reshape(rows // 128, 128),
        positions.reshape(rows // 128, 128),
    )
    return divergence.reshape(rows), grad


def solution(mesh):
    return jax.shard_map(
        shards,
        mesh=mesh,
        in_specs=(
            P("ctx", "vocab"),
            P("ctx", None),
            P("ctx", None),
            P("vocab"),
            P("vocab", None),
            P(),
            P("ctx", "vocab"),
            P(),
            P("ctx", "vocab"),
            P(None, "vocab"),
            P(None, "vocab"),
            P("ctx"),
            P("ctx"),
            P("ctx"),
        ),
        out_specs=(P("ctx"), P("vocab", "ctx")),
        check_vma=False,
    )
```

```python
import functools

import jax
import jax.numpy as jnp
from jax import lax
from jax.experimental import pallas as pl
from jax.experimental.pallas import tpu as pltpu
from jax.sharding import PartitionSpec as P

MESH = pl.DeviceIdType.MESH
BF = jnp.bfloat16
F32 = jnp.float32
HEAD_DIM = 64
WINDOW = 128
SIDE = 4
GROUP = SIDE * SIDE
HALVES = 2
NT = (((1,), (1,)), ((), ()))


class Pool:
    def __init__(self, send_sems, recv_sems):
        self.send_sems, self.recv_sems = send_sems, recv_sems
        self.copies = []

    def start(self, src, dst, device):
        at = len(self.copies)
        copy = pltpu.make_async_remote_copy(
            src_ref=src,
            dst_ref=dst,
            send_sem=self.send_sems.at[at],
            recv_sem=self.recv_sems.at[at],
            device_id=device,
            device_id_type=MESH,
        )
        copy.start()
        self.copies.append(copy)
        return copy


def add_into(dst, src):
    dst[...] = (dst[...].astype(F32) + src[...].astype(F32)).astype(BF)


class Gather:
    def __init__(self, pool, place, buf, half):
        self.pool, self.place, self.buf, self.half = pool, place, buf, half

    def piece(self, da, db):
        return self.buf.at[self.place.block(da, db)]

    def send(self, piece, da, db):
        return self.pool.start(piece, piece, self.place.device(da, db))

    def s0(self):
        own = self.piece(0, 0)
        self.ap, self.am = self.send(own, 1, 0), self.send(own, -1, 0)
        self.bp0, self.bm0 = self.send(own, 0, 1), self.send(own, 0, -1)

    def s1(self):
        self.ap.wait_recv()
        got = self.piece(-1, 0)
        if self.half == 0:
            self.a2 = self.send(got, 1, 0)
        self.bp1, self.bm1 = self.send(got, 0, 1), self.send(got, 0, -1)

    def s2(self):
        self.am.wait_recv()
        got = self.piece(1, 0)
        if self.half == 1:
            self.a2 = self.send(got, -1, 0)
        self.bp2, self.bm2 = self.send(got, 0, 1), self.send(got, 0, -1)

    def s3(self):
        self.a2.wait_recv()
        got = self.piece(2, 0)
        self.bp3, self.bm3 = self.send(got, 0, 1), self.send(got, 0, -1)

    def s4(self):
        self.bp0.wait_recv()
        self.f0 = self.send(self.piece(0, -1), 0, 1)

    def s5(self):
        self.bp1.wait_recv()
        self.f1 = self.send(self.piece(-1, -1), 0, 1)

    def s6(self):
        self.bm2.wait_recv()
        self.f2 = self.send(self.piece(1, 1), 0, -1)

    def s7(self):
        self.bm3.wait_recv()
        self.f3 = self.send(self.piece(2, 1), 0, -1)

    def s8(self):
        for copy in (self.bm0, self.bm1, self.bp2, self.bp3, self.f0, self.f1, self.f2, self.f3):
            copy.wait_recv()


class Scatter:
    def __init__(self, pool, place, x, tp, tm, fp, fm, y, fa):
        self.pool, self.place = pool, place
        self.x, self.tp, self.tm, self.fp, self.fm = x, tp, tm, fp, fm
        self.y, self.fa = y, fa

    def group(self, db, first, count):
        return self.x.at[pl.ds(SIDE * self.place.along_b(db) + first, count)]

    def send(self, src, dst, db):
        return self.pool.start(src, dst, self.place.device(0, db))

    def far(self):
        self.c_tp = self.send(self.group(2, 0, 2), self.tp, 1)
        self.c_tm = self.send(self.group(2, 2, 2), self.tm, -1)

    def near_up(self):
        self.c_fp2 = self.send(self.group(1, 2, 2), self.fp.at[pl.ds(2, 2)], 1)

    def near_down(self):
        self.c_fm0 = self.send(self.group(-1, 0, 2), self.fm.at[pl.ds(0, 2)], -1)

    def pass_on(self):
        self.c_tp.wait_recv()
        add_into(self.group(1, 0, 2), self.tp)
        self.c_fp0 = self.send(self.group(1, 0, 2), self.fp.at[pl.ds(0, 2)], 1)
        self.c_tm.wait_recv()
        add_into(self.group(-1, 2, 2), self.tm)
        self.c_fm2 = self.send(self.group(-1, 2, 2), self.fm.at[pl.ds(2, 2)], -1)

    def here(self, i):
        return (
            self.x[SIDE * self.place.b + i].astype(F32)
            + self.fp[i].astype(F32)
            + self.fm[i].astype(F32)
        )

    def turn(self):
        for copy in (self.c_fp2, self.c_fm0, self.c_fp0, self.c_fm2):
            copy.wait_recv()
        self.c_fa = []
        for slot, da in enumerate((2, 1, -1)):
            to = self.place.along_a(da)
            self.y[slot] = self.here(to).astype(BF)
            self.c_fa.append(
                self.pool.start(self.y.at[slot], self.fa.at[slot], self.place.device(da, 0))
            )

    def result(self):
        total = self.here(self.place.a)
        for slot in range(SIDE - 1):
            self.c_fa[slot].wait_recv()
            total = total + self.fa[slot].astype(F32)
        return total


class Place:
    def __init__(self):
        self.ctx, self.vocab = lax.axis_index("ctx"), lax.axis_index("vocab")
        self.z, self.x = self.vocab // SIDE, lax.rem(self.vocab, SIDE)
        self.core = lax.rem(self.ctx, 2)
        self.a = self.x * (1 - self.core) + self.z * self.core
        self.b = self.z * (1 - self.core) + self.x * self.core

    def along_a(self, da):
        return lax.rem(self.a + (da + SIDE), SIDE)

    def along_b(self, db):
        return lax.rem(self.b + (db + SIDE), SIDE)

    def block(self, da, db):
        return SIDE * self.along_b(db) + self.along_a(da)

    def device(self, da, db):
        a, b = self.along_a(da), self.along_b(db)
        return (self.ctx, a * (1 + 3 * self.core) + b * (4 - 3 * self.core))

    def block_of(self, vocab):
        turned = SIDE * lax.rem(vocab, SIDE) + vocab // SIDE
        return vocab * (1 - self.core) + turned * self.core


def column(row):
    return jnp.broadcast_to(row, (128, 128)).T


def kernel(
    queries_hbm,
    key_rows_hbm,
    value_rows_hbm,
    sinks,
    out_weight_hbm,
    bias,
    residual_hbm,
    gain,
    policy_hidden_hbm,
    ref_head_hbm,
    policy_head_hbm,
    token_ids,
    advantages,
    positions,
    divergence_out,
    grad_out,
    out_weight,
    ref_head,
    policy_head,
    head_blocks,
    queries,
    key_pair,
    value_pair,
    policy_turned,
    residual_turned,
    policy_hidden,
    residual,
    kv,
    attended,
    land_policy,
    land_residual,
    residual_own,
    policy_rows,
    normed_rows,
    partial_rows,
    policy_logits,
    ref_logits,
    logit_grad,
    grad_parts,
    pol_max,
    pol_sum,
    stats,
    p_tp,
    p_tm,
    p_fp,
    p_fm,
    p_y,
    p_fa,
    g_tp,
    g_tm,
    g_fp,
    g_fm,
    g_y,
    g_fa,
    local_sems,
    send_sems,
    recv_sems,
    policy_sems,
    residual_sems,
    stat_sems,
):
    rows, width = attended.shape[0], out_weight.shape[0]
    half_rows = rows // HALVES
    piece = half_rows // GROUP
    share = land_policy.shape[3]
    vocab_here = ref_head.shape[1]
    place = Place()
    me = place.vocab
    own = place.block(0, 0)

    kv_lanes = pl.ds(pl.multiple_of(place.z * 128, 128), 128)
    loads = [
        pltpu.make_async_copy(src, dst, local_sems.at[i])
        for i, (src, dst) in enumerate(
            (
                (policy_hidden_hbm, policy_turned),
                (key_rows_hbm.at[:, kv_lanes], key_pair),
                (value_rows_hbm.at[:, kv_lanes], value_pair),
                (queries_hbm, queries),
                (out_weight_hbm, out_weight),
                (residual_hbm, residual_turned),
                (policy_head_hbm, policy_head),
                (ref_head_hbm, ref_head),
            )
        )
    ]
    l_policy, l_key, l_value, l_query, l_out, l_residual, l_policy_head, l_ref_head = loads
    for load in loads:
        load.start()

    barrier = pltpu.get_barrier_semaphore()
    ctx_count = lax.axis_size("ctx")
    next_ctx = lax.rem(place.ctx + 1, ctx_count)
    last_ctx = lax.rem(place.ctx + ctx_count - 1, ctx_count)
    for other in (next_ctx, last_ctx):
        pl.semaphore_signal(barrier, inc=1, device_id=(other, me), device_id_type=MESH)

    def greet(t, carry):
        pl.semaphore_signal(
            barrier,
            inc=1,
            device_id=(place.ctx, lax.rem(me + t, GROUP)),
            device_id_type=MESH,
        )
        return carry

    lax.fori_loop(1, GROUP, greet, 0)

    own_rows = pl.ds(pl.multiple_of(own * piece, piece), piece)

    def turn_over(source, out, land):
        for h in range(HALVES):
            out[h] = source[:, h * half_rows : (h + 1) * half_rows].T
        land[me] = out[:, own_rows, :]

    l_policy.wait()
    turn_over(policy_turned, policy_hidden, land_policy)

    upper = lax.rem(me // 2, 2) == 1
    l_key.wait()
    l_value.wait()
    for pair, lane in ((key_pair, 0), (value_pair, HEAD_DIM)):
        kv[pl.ds(WINDOW, rows), lane : lane + HEAD_DIM] = jnp.where(
            upper, pair[:, HEAD_DIM:], pair[:, :HEAD_DIM]
        )

    pl.semaphore_wait(barrier, GROUP - 1 + 2)

    pool = Pool(send_sems, recv_sems)
    halo = pool.start(kv.at[pl.ds(rows, WINDOW)], kv.at[pl.ds(0, WINDOW)], (next_ctx, me))

    def spread(source, land, sems, t):
        to = lax.rem(me + t, GROUP)
        block = pl.ds(pl.multiple_of(place.block_of(to) * piece, piece), piece)
        return pltpu.make_async_remote_copy(
            src_ref=source.at[:, block, :],
            dst_ref=land.at[me],
            send_sem=sems.at[0, t - 1],
            recv_sem=sems.at[1, t - 1],
            device_id=(place.ctx, to),
            device_id_type=MESH,
        )

    def each_peer(act):
        def body(t, carry):
            act(t)
            return carry

        lax.fori_loop(1, GROUP, body, 0)

    each_peer(lambda t: spread(policy_hidden, land_policy, policy_sems, t).start())

    def attend(block):
        at = block * WINDOW
        keys = kv[at : at + 2 * WINDOW, :HEAD_DIM]
        values = kv[at : at + 2 * WINDOW, HEAD_DIM:]
        query = queries[at : at + WINDOW, :]
        heads = query.shape[1] // HEAD_DIM
        offsets = (
            lax.broadcasted_iota(jnp.int32, (WINDOW, 2 * WINDOW), 0)
            + WINDOW
            - lax.broadcasted_iota(jnp.int32, (WINDOW, 2 * WINDOW), 1)
        )
        where_at = column(positions[block : block + 1, :].astype(F32))
        where_at = jnp.concatenate([where_at, where_at], axis=1)
        allowed = (offsets >= 0) & (offsets < WINDOW) & (where_at >= offsets.astype(F32))
        mixed = []
        for h in range(heads):
            scores = (
                lax.dot_general(
                    query[:, h * HEAD_DIM : (h + 1) * HEAD_DIM],
                    keys,
                    NT,
                    preferred_element_type=F32,
                )
                * HEAD_DIM**-0.5
            )
            scores = jnp.where(allowed, scores, -jnp.inf)
            sink = sinks[h]
            peak = jnp.maximum(jnp.max(scores, axis=1, keepdims=True), sink)
            raised = jnp.exp(scores - peak)
            total = jnp.sum(raised, axis=1, keepdims=True) + jnp.exp(sink - peak)
            weights = (raised / total).astype(BF)
            mixed.append(jnp.dot(weights, values, preferred_element_type=F32).astype(BF))
        attended[at : at + WINDOW, :] = jnp.concatenate(mixed, axis=1)

    def project(half):
        rows_in = attended[half * half_rows : (half + 1) * half_rows, :]
        for start in range(0, width, 512):
            stop = min(start + 512, width)
            partial_rows[half, :, :, start:stop] = (
                lax.dot_general(
                    rows_in, out_weight[start:stop, :], NT, preferred_element_type=F32
                )
                .astype(BF)
                .reshape(GROUP, piece, stop - start)
            )

    policy_ag = [Gather(pool, place, policy_rows.at[h], h) for h in range(HALVES)]
    normed_ag = [Gather(pool, place, normed_rows.at[h], h) for h in range(HALVES)]

    def scatter(x, bufs, h):
        return Scatter(pool, place, x.at[h], *(buf.at[h] for buf in bufs))

    p_bufs = (p_tp, p_tm, p_fp, p_fm, p_y, p_fa)
    g_bufs = (g_tp, g_tm, g_fp, g_fm, g_y, g_fa)
    partial_rs = [scatter(partial_rows, p_bufs, h) for h in range(HALVES)]
    grad_rs = [scatter(grad_parts, g_bufs, h) for h in range(HALVES)]

    def join(land, h):
        return jnp.concatenate([land[v, h] for v in range(GROUP)], axis=1)

    def normalise(h):
        projected = partial_rs[h].result() + bias[...].reshape(1, width)
        hidden = (residual_own[h].astype(F32) + projected).astype(BF)
        wide = hidden.astype(F32)
        spread_of = jnp.sum(wide * wide, axis=1, keepdims=True) * (1.0 / width)
        normed_rows[h, own] = (wide * lax.rsqrt(spread_of + 1e-05) * gain[...].reshape(1, width)).astype(BF)

    def logits(rows_of, head, out, h, tile, tiles=3):
        cols = slice(tile * (vocab_here // tiles), (tile + 1) * (vocab_here // tiles))
        lhs = rows_of[h].reshape(half_rows, width)
        out[h, :, cols] = jnp.dot(lhs, head[:, cols], preferred_element_type=F32)

    def policy_stats(h):
        top = jnp.max(policy_logits[h], axis=1, keepdims=True)
        pol_max[h] = jnp.broadcast_to(top, pol_max.shape[1:])
        pol_sum[h] = jnp.broadcast_to(
            jnp.sum(jnp.exp(policy_logits[h] - top), axis=1, keepdims=True), pol_sum.shape[1:]
        )

    def stat_copy(h, t):
        to = lax.rem(me + t, GROUP)
        return pltpu.make_async_remote_copy(
            src_ref=stats.at[h, me],
            dst_ref=stats.at[h, me],
            send_sem=stat_sems.at[h, 0, t - 1],
            recv_sem=stat_sems.at[h, 1, t - 1],
            device_id=(place.ctx, to),
            device_id_type=MESH,
        )

    def send_stats(h):
        top = jnp.max(ref_logits[h], axis=1, keepdims=True)
        total = jnp.sum(jnp.exp(ref_logits[h] - top), axis=1, keepdims=True)
        pol_top = pol_max[h][:, :1]
        gap = jnp.sum(
            jnp.exp(policy_logits[h] - pol_top) * (policy_logits[h] - ref_logits[h]),
            axis=1,
            keepdims=True,
        )
        lane = lax.broadcasted_iota(jnp.int32, (half_rows, 128), 1)
        packed = jnp.where(lane == 0, pol_max[h], pol_sum[h])
        packed = jnp.where(lane == 2, top, packed)
        packed = jnp.where(lane == 3, total, packed)
        packed = jnp.where(lane == 4, gap, packed)
        stats[h, me] = packed.T[:8, :]
        each_peer(lambda t: stat_copy(h, t).start())

    def loss_gradient(h):
        each_peer(lambda t: stat_copy(h, t).wait_recv())
        pol_tops, pol_sums = stats[h, :, 0, :], stats[h, :, 1, :]
        ref_tops, ref_sums = stats[h, :, 2, :], stats[h, :, 3, :]
        pol_top = jnp.max(pol_tops, axis=0, keepdims=True)
        ref_top = jnp.max(ref_tops, axis=0, keepdims=True)
        scale = jnp.exp(pol_tops - pol_top)
        pol_total = jnp.sum(pol_sums * scale, axis=0, keepdims=True)
        gap = jnp.sum(stats[h, :, 4, :] * scale, axis=0, keepdims=True) / pol_total
        ref_total = jnp.sum(ref_sums * jnp.exp(ref_tops - ref_top), axis=0, keepdims=True)
        log_pol = pol_top + jnp.log(pol_total)
        log_ref = ref_top + jnp.log(ref_total)
        divergence = gap - log_pol + log_ref
        for part in range(half_rows // 128):
            lanes = slice(part * 128, (part + 1) * 128)
            at = h * (half_rows // 128) + part
            here = slice(part * 128, (part + 1) * 128)
            divergence_out[at : at + 1, :] = divergence[:, lanes]
            adv_row = advantages[at : at + 1, :]
            log_col = column(log_pol[:, lanes])
            add_col = column(adv_row - gap[:, lanes])
            adv_col = column(adv_row)
            tok_col = column(
                (token_ids[at : at + 1, :] - me * vocab_here).astype(F32)
            )
            for chunk in range(0, vocab_here, 128):
                cols = slice(chunk, chunk + 128)
                ids = (lax.broadcasted_iota(jnp.int32, (128, 128), 1) + chunk).astype(F32)
                pol = policy_logits[h, here, cols]
                prob = jnp.exp(pol - log_col)
                value = prob * (pol - ref_logits[h, here, cols] + add_col)
                logit_grad[h, here, cols] = (
                    value - jnp.where(ids == tok_col, adv_col, 0.0)
                ).astype(BF)

    def gradient(h, db):
        at = pl.ds(SIDE * place.along_b(db), SIDE)
        block_rows = head_blocks.shape[1]
        lhs = head_blocks[at].reshape(SIDE * block_rows, vocab_here)
        grad_parts[h, at] = (
            lax.dot_general(lhs, logit_grad[h], NT, preferred_element_type=F32)
            .astype(BF)
            .reshape(SIDE, block_rows, half_rows)
        )

    def finish(h):
        grad_out[:, h * half_rows : (h + 1) * half_rows] = grad_rs[h].result()[:share, :]

    one, two = 1, 0
    l_query.wait()
    attend(2)
    attend(3)
    l_out.wait()
    project(one)
    partial_rs[one].far()
    partial_rs[one].near_up()
    partial_rs[one].near_down()
    each_peer(lambda t: spread(policy_hidden, land_policy, policy_sems, t).wait_recv())
    policy_rows[one, own] = join(land_policy, one)
    policy_ag[one].s0()
    halo.wait_recv()
    attend(0)
    attend(1)
    project(two)
    partial_rs[two].far()
    partial_rs[two].near_up()
    partial_rs[two].near_down()
    l_residual.wait()
    turn_over(residual_turned, residual, land_residual)
    each_peer(lambda t: spread(residual, land_residual, residual_sems, t).start())
    partial_rs[one].pass_on()
    policy_ag[one].s1()
    policy_ag[one].s2()
    policy_rows[two, own] = join(land_policy, two)
    partial_rs[two].pass_on()
    policy_ag[one].s4()
    policy_ag[one].s3()
    each_peer(lambda t: spread(residual, land_residual, residual_sems, t).wait_recv())
    residual_own[one] = join(land_residual, one)
    partial_rs[one].turn()
    residual_own[two] = join(land_residual, two)
    policy_ag[one].s5()
    policy_ag[one].s6()
    normalise(one)
    normed_ag[one].s0()
    partial_rs[two].turn()
    policy_ag[one].s7()
    policy_ag[two].s0()
    normed_ag[one].s1()
    normed_ag[one].s2()
    normalise(two)
    normed_ag[two].s0()
    normed_ag[one].s4()
    normed_ag[one].s3()
    policy_ag[two].s1()
    policy_ag[two].s2()
    l_policy_head.wait()
    for d in range(GROUP):
        head_blocks[place.block_of(d), :share, :] = policy_head[d * share : (d + 1) * share, :]
    normed_ag[one].s5()
    normed_ag[one].s6()
    normed_ag[one].s7()
    policy_ag[one].s8()
    logits(policy_rows, policy_head, policy_logits, one, 0)
    policy_ag[two].s4()
    policy_ag[two].s3()
    normed_ag[two].s1()
    normed_ag[two].s2()
    logits(policy_rows, policy_head, policy_logits, one, 1)
    policy_ag[two].s5()
    policy_ag[two].s6()
    policy_ag[two].s7()
    normed_ag[two].s4()
    normed_ag[two].s3()
    logits(policy_rows, policy_head, policy_logits, one, 2)
    normed_ag[two].s5()
    normed_ag[two].s6()
    policy_stats(one)
    normed_ag[two].s7()
    normed_ag[one].s8()
    l_ref_head.wait()
    for tile in range(3):
        logits(normed_rows, ref_head, ref_logits, one, tile)
    send_stats(one)
    policy_ag[two].s8()
    logits(policy_rows, policy_head, policy_logits, two, 0)
    logits(policy_rows, policy_head, policy_logits, two, 1)
    loss_gradient(one)
    gradient(one, 2)
    grad_rs[one].far()
    gradient(one, 1)
    grad_rs[one].near_up()
    gradient(one, -1)
    grad_rs[one].near_down()
    logits(policy_rows, policy_head, policy_logits, two, 2)
    grad_rs[one].pass_on()
    normed_ag[two].s8()
    for tile in range(3):
        logits(normed_rows, ref_head, ref_logits, two, tile)
    policy_stats(two)
    send_stats(two)
    gradient(one, 0)
    grad_rs[one].turn()
    loss_gradient(two)
    gradient(two, 2)
    grad_rs[two].far()
    gradient(two, 1)
    grad_rs[two].near_up()
    gradient(two, -1)
    grad_rs[two].near_down()
    gradient(two, 0)
    finish(one)
    grad_rs[two].pass_on()
    grad_rs[two].turn()
    finish(two)

    for copy in pool.copies:
        copy.wait_send()
    each_peer(lambda t: spread(policy_hidden, land_policy, policy_sems, t).wait_send())
    each_peer(lambda t: spread(residual, land_residual, residual_sems, t).wait_send())
    for h in range(HALVES):
        each_peer(lambda t: stat_copy(h, t).wait_send())


def shards(
    queries,
    key_rows,
    value_rows,
    sink_logits,
    out_weight,
    out_bias,
    residual,
    norm_gain,
    policy_hidden,
    ref_head,
    policy_head,
    token_ids,
    advantages,
    positions,
):
    rows, heads_width = queries.shape
    share = residual.shape[1]
    width, vocab_here = ref_head.shape
    half_rows = rows // HALVES
    piece = half_rows // GROUP
    block_rows = -(-share // 16) * 16
    copies = 1 + HALVES * 2 * (15 + 9)

    def sums(block):
        return [
            pltpu.VMEM((HALVES, lead, *block), BF)
            for lead in (2, 2, SIDE, SIDE, SIDE - 1, SIDE - 1)
        ]

    vmem, hbm = (pl.BlockSpec(memory_space=space) for space in (pltpu.VMEM, pl.ANY))
    smem = pl.BlockSpec(memory_space=pltpu.SMEM)
    divergence, grad = pl.pallas_call(
        kernel,
        out_shape=(
            jax.ShapeDtypeStruct((rows // 128, 128), F32),
            jax.ShapeDtypeStruct((share, rows), F32),
        ),
        in_specs=[
            hbm, hbm, hbm, smem, hbm, vmem, hbm, vmem, hbm, hbm, hbm, vmem, vmem, vmem,
        ],
        out_specs=(vmem, vmem),
        scratch_shapes=[
            pltpu.VMEM((width, heads_width), BF),
            pltpu.VMEM((width, vocab_here), BF),
            pltpu.VMEM((width, vocab_here), BF),
            pltpu.VMEM((GROUP, block_rows, vocab_here), BF),
            pltpu.VMEM((rows, heads_width), BF),
            pltpu.VMEM((rows, 2 * HEAD_DIM), BF),
            pltpu.VMEM((rows, 2 * HEAD_DIM), BF),
            pltpu.VMEM((share, rows), BF),
            pltpu.VMEM((share, rows), BF),
            pltpu.VMEM((HALVES, half_rows, share), BF),
            pltpu.VMEM((HALVES, half_rows, share), BF),
            pltpu.VMEM((WINDOW + rows, 2 * HEAD_DIM), BF),
            pltpu.VMEM((rows, heads_width), BF),
            pltpu.VMEM((GROUP, HALVES, piece, share), BF),
            pltpu.VMEM((GROUP, HALVES, piece, share), BF),
            pltpu.VMEM((HALVES, piece, width), BF),
            pltpu.VMEM((HALVES, GROUP, piece, width), BF),
            pltpu.VMEM((HALVES, GROUP, piece, width), BF),
            pltpu.VMEM((HALVES, GROUP, piece, width), BF),
            pltpu.VMEM((HALVES, half_rows, vocab_here), F32),
            pltpu.VMEM((HALVES, half_rows, vocab_here), F32),
            pltpu.VMEM((HALVES, half_rows, vocab_here), BF),
            pltpu.VMEM((HALVES, GROUP, block_rows, half_rows), BF),
            pltpu.VMEM((HALVES, half_rows, 128), F32),
            pltpu.VMEM((HALVES, half_rows, 128), F32),
            pltpu.VMEM((HALVES, GROUP, 8, half_rows), F32),
            *sums((piece, width)),
            *sums((block_rows, half_rows)),
            pltpu.SemaphoreType.DMA((8,)),
            pltpu.SemaphoreType.DMA((copies,)),
            pltpu.SemaphoreType.DMA((copies,)),
            pltpu.SemaphoreType.DMA((2, GROUP - 1)),
            pltpu.SemaphoreType.DMA((2, GROUP - 1)),
            pltpu.SemaphoreType.DMA((HALVES, 2, GROUP - 1)),
        ],
        compiler_params=pltpu.CompilerParams(
            collective_id=0, has_side_effects=True, vmem_limit_bytes=62 << 20
        ),
    )(
        queries,
        key_rows,
        value_rows,
        sink_logits,
        out_weight.T,
        out_bias,
        residual.T,
        norm_gain,
        policy_hidden.T,
        ref_head,
        policy_head,
        token_ids.reshape(rows // 128, 128),
        advantages.reshape(rows // 128, 128),
        positions.reshape(rows // 128, 128),
    )
    return divergence.reshape(rows), grad


def solution(mesh):
    return jax.shard_map(
        shards,
        mesh=mesh,
        in_specs=(
            P("ctx", "vocab"),
            P("ctx", None),
            P("ctx", None),
            P("vocab"),
            P("vocab", None),
            P(),
            P("ctx", "vocab"),
            P(),
            P("ctx", "vocab"),
            P(None, "vocab"),
            P(None, "vocab"),
            P("ctx"),
            P("ctx"),
            P("ctx"),
        ),
        out_specs=(P("ctx"), P("vocab", "ctx")),
        check_vma=False,
    )
```

```python
import functools

import jax
import jax.numpy as jnp
from jax import lax
from jax.experimental import pallas as pl
from jax.experimental.pallas import tpu as pltpu
from jax.sharding import PartitionSpec as P

MESH = pl.DeviceIdType.MESH
BF = jnp.bfloat16
F32 = jnp.float32
HEAD_DIM = 64
WINDOW = 128
SIDE = 4
GROUP = SIDE * SIDE
HALVES = 2
NT = (((1,), (1,)), ((), ()))


class Pool:
    def __init__(self, send_sems, recv_sems):
        self.send_sems, self.recv_sems = send_sems, recv_sems
        self.copies = []

    def start(self, src, dst, device):
        at = len(self.copies)
        copy = pltpu.make_async_remote_copy(
            src_ref=src,
            dst_ref=dst,
            send_sem=self.send_sems.at[at],
            recv_sem=self.recv_sems.at[at],
            device_id=device,
            device_id_type=MESH,
        )
        copy.start()
        self.copies.append(copy)
        return copy


def add_into(dst, src):
    dst[...] = (dst[...].astype(F32) + src[...].astype(F32)).astype(BF)


class Gather:
    def __init__(self, pool, place, buf, half):
        self.pool, self.place, self.buf, self.half = pool, place, buf, half

    def piece(self, da, db):
        return self.buf.at[self.place.block(da, db)]

    def send(self, piece, da, db):
        return self.pool.start(piece, piece, self.place.device(da, db))

    def s0(self):
        own = self.piece(0, 0)
        self.ap, self.am = self.send(own, 1, 0), self.send(own, -1, 0)
        self.bp0, self.bm0 = self.send(own, 0, 1), self.send(own, 0, -1)

    def s1(self):
        self.ap.wait_recv()
        got = self.piece(-1, 0)
        if self.half == 0:
            self.a2 = self.send(got, 1, 0)
        self.bp1, self.bm1 = self.send(got, 0, 1), self.send(got, 0, -1)

    def s2(self):
        self.am.wait_recv()
        got = self.piece(1, 0)
        if self.half == 1:
            self.a2 = self.send(got, -1, 0)
        self.bp2, self.bm2 = self.send(got, 0, 1), self.send(got, 0, -1)

    def s3(self):
        self.a2.wait_recv()
        got = self.piece(2, 0)
        self.bp3, self.bm3 = self.send(got, 0, 1), self.send(got, 0, -1)

    def s4(self):
        self.bp0.wait_recv()
        self.f0 = self.send(self.piece(0, -1), 0, 1)

    def s5(self):
        self.bp1.wait_recv()
        self.f1 = self.send(self.piece(-1, -1), 0, 1)

    def s6(self):
        self.bm2.wait_recv()
        self.f2 = self.send(self.piece(1, 1), 0, -1)

    def s7(self):
        self.bm3.wait_recv()
        self.f3 = self.send(self.piece(2, 1), 0, -1)

    def s8(self):
        for copy in (self.bm0, self.bm1, self.bp2, self.bp3, self.f0, self.f1, self.f2, self.f3):
            copy.wait_recv()


class Scatter:
    def __init__(self, pool, place, x, tp, tm, fp, fm, y, fa):
        self.pool, self.place = pool, place
        self.x, self.tp, self.tm, self.fp, self.fm = x, tp, tm, fp, fm
        self.y, self.fa = y, fa

    def group(self, db, first, count):
        return self.x.at[pl.ds(SIDE * self.place.along_b(db) + first, count)]

    def send(self, src, dst, db):
        return self.pool.start(src, dst, self.place.device(0, db))

    def far(self):
        self.c_tp = self.send(self.group(2, 0, 2), self.tp, 1)
        self.c_tm = self.send(self.group(2, 2, 2), self.tm, -1)

    def near_up(self):
        self.c_fp2 = self.send(self.group(1, 2, 2), self.fp.at[pl.ds(2, 2)], 1)

    def near_down(self):
        self.c_fm0 = self.send(self.group(-1, 0, 2), self.fm.at[pl.ds(0, 2)], -1)

    def pass_up(self):
        self.c_tp.wait_recv()
        add_into(self.group(1, 0, 2), self.tp)
        self.c_fp0 = self.send(self.group(1, 0, 2), self.fp.at[pl.ds(0, 2)], 1)

    def pass_down(self):
        self.c_tm.wait_recv()
        add_into(self.group(-1, 2, 2), self.tm)
        self.c_fm2 = self.send(self.group(-1, 2, 2), self.fm.at[pl.ds(2, 2)], -1)

    def here(self, i):
        return (
            self.x[SIDE * self.place.b + i].astype(F32)
            + self.fp[i].astype(F32)
            + self.fm[i].astype(F32)
        )

    def turn(self):
        for copy in (self.c_fp2, self.c_fm0, self.c_fp0, self.c_fm2):
            copy.wait_recv()
        self.c_fa = []
        for slot, da in enumerate((2, 1, -1)):
            to = self.place.along_a(da)
            self.y[slot] = self.here(to).astype(BF)
            self.c_fa.append(
                self.pool.start(self.y.at[slot], self.fa.at[slot], self.place.device(da, 0))
            )

    def result(self):
        total = self.here(self.place.a)
        for slot in range(SIDE - 1):
            self.c_fa[slot].wait_recv()
            total = total + self.fa[slot].astype(F32)
        return total


class Place:
    def __init__(self):
        self.ctx, self.vocab = lax.axis_index("ctx"), lax.axis_index("vocab")
        self.z, self.x = self.vocab // SIDE, lax.rem(self.vocab, SIDE)
        self.core = lax.rem(self.ctx, 2)
        self.a = self.x * (1 - self.core) + self.z * self.core
        self.b = self.z * (1 - self.core) + self.x * self.core

    def along_a(self, da):
        return lax.rem(self.a + (da + SIDE), SIDE)

    def along_b(self, db):
        return lax.rem(self.b + (db + SIDE), SIDE)

    def block(self, da, db):
        return SIDE * self.along_b(db) + self.along_a(da)

    def device(self, da, db):
        a, b = self.along_a(da), self.along_b(db)
        return (self.ctx, a * (1 + 3 * self.core) + b * (4 - 3 * self.core))

    def block_of(self, vocab):
        turned = SIDE * lax.rem(vocab, SIDE) + vocab // SIDE
        return vocab * (1 - self.core) + turned * self.core


def column(row):
    return jnp.broadcast_to(row, (128, 128)).T


def kernel(
    queries_hbm,
    key_rows_hbm,
    value_rows_hbm,
    sinks,
    out_weight_hbm,
    bias,
    residual_hbm,
    gain,
    policy_hidden_hbm,
    ref_head_hbm,
    policy_head_hbm,
    token_ids,
    advantages,
    positions,
    divergence_out,
    grad_out,
    out_weight,
    ref_head,
    policy_head,
    head_blocks,
    queries,
    key_pair,
    value_pair,
    policy_turned,
    residual_turned,
    policy_hidden,
    residual,
    kv,
    attended,
    land_policy,
    land_residual,
    residual_own,
    policy_rows,
    normed_rows,
    partial_rows,
    policy_logits,
    ref_logits,
    logit_grad,
    grad_parts,
    pol_max,
    pol_sum,
    stats,
    p_tp,
    p_tm,
    p_fp,
    p_fm,
    p_y,
    p_fa,
    g_tp,
    g_tm,
    g_fp,
    g_fm,
    g_y,
    g_fa,
    local_sems,
    send_sems,
    recv_sems,
    policy_sems,
    residual_sems,
    stat_sems,
):
    rows, width = attended.shape[0], out_weight.shape[0]
    half_rows = rows // HALVES
    piece = half_rows // GROUP
    share = land_policy.shape[3]
    vocab_here = ref_head.shape[1]
    place = Place()
    me = place.vocab
    own = place.block(0, 0)

    kv_lanes = pl.ds(pl.multiple_of(place.z * 128, 128), 128)
    loads = [
        pltpu.make_async_copy(src, dst, local_sems.at[i])
        for i, (src, dst) in enumerate(
            (
                (policy_hidden_hbm, policy_turned),
                (key_rows_hbm.at[:, kv_lanes], key_pair),
                (value_rows_hbm.at[:, kv_lanes], value_pair),
                (queries_hbm, queries),
                (out_weight_hbm, out_weight),
                (residual_hbm, residual_turned),
                (policy_head_hbm, policy_head),
                (ref_head_hbm, ref_head),
            )
        )
    ]
    l_policy, l_key, l_value, l_query, l_out, l_residual, l_policy_head, l_ref_head = loads
    for load in loads:
        load.start()

    barrier = pltpu.get_barrier_semaphore()
    ctx_count = lax.axis_size("ctx")
    next_ctx = lax.rem(place.ctx + 1, ctx_count)
    last_ctx = lax.rem(place.ctx + ctx_count - 1, ctx_count)
    for other in (next_ctx, last_ctx):
        pl.semaphore_signal(barrier, inc=1, device_id=(other, me), device_id_type=MESH)

    def greet(t, carry):
        pl.semaphore_signal(
            barrier,
            inc=1,
            device_id=(place.ctx, lax.rem(me + t, GROUP)),
            device_id_type=MESH,
        )
        return carry

    lax.fori_loop(1, GROUP, greet, 0)

    own_rows = pl.ds(pl.multiple_of(own * piece, piece), piece)

    def turn_over(source, out, land):
        for h in range(HALVES):
            out[h] = source[:, h * half_rows : (h + 1) * half_rows].T
        land[me] = out[:, own_rows, :]

    l_policy.wait()
    turn_over(policy_turned, policy_hidden, land_policy)

    upper = lax.rem(me // 2, 2) == 1
    l_key.wait()
    l_value.wait()
    for pair, lane in ((key_pair, 0), (value_pair, HEAD_DIM)):
        kv[pl.ds(WINDOW, rows), lane : lane + HEAD_DIM] = jnp.where(
            upper, pair[:, HEAD_DIM:], pair[:, :HEAD_DIM]
        )

    pl.semaphore_wait(barrier, GROUP - 1 + 2)

    pool = Pool(send_sems, recv_sems)
    halo = pool.start(kv.at[pl.ds(rows, WINDOW)], kv.at[pl.ds(0, WINDOW)], (next_ctx, me))

    def spread(source, land, sems, t):
        to = lax.rem(me + t, GROUP)
        block = pl.ds(pl.multiple_of(place.block_of(to) * piece, piece), piece)
        return pltpu.make_async_remote_copy(
            src_ref=source.at[:, block, :],
            dst_ref=land.at[me],
            send_sem=sems.at[0, t - 1],
            recv_sem=sems.at[1, t - 1],
            device_id=(place.ctx, to),
            device_id_type=MESH,
        )

    def each_peer(act):
        def body(t, carry):
            act(t)
            return carry

        lax.fori_loop(1, GROUP, body, 0)

    each_peer(lambda t: spread(policy_hidden, land_policy, policy_sems, t).start())

    def attend(block):
        at = block * WINDOW
        keys = kv[at : at + 2 * WINDOW, :HEAD_DIM]
        values = kv[at : at + 2 * WINDOW, HEAD_DIM:]
        query = queries[at : at + WINDOW, :]
        heads = query.shape[1] // HEAD_DIM
        offsets = (
            lax.broadcasted_iota(jnp.int32, (WINDOW, 2 * WINDOW), 0)
            + WINDOW
            - lax.broadcasted_iota(jnp.int32, (WINDOW, 2 * WINDOW), 1)
        )
        where_at = column(positions[block : block + 1, :].astype(F32))
        where_at = jnp.concatenate([where_at, where_at], axis=1)
        allowed = (offsets >= 0) & (offsets < WINDOW) & (where_at >= offsets.astype(F32))
        mixed = []
        for h in range(heads):
            scores = (
                lax.dot_general(
                    query[:, h * HEAD_DIM : (h + 1) * HEAD_DIM],
                    keys,
                    NT,
                    preferred_element_type=F32,
                )
                * HEAD_DIM**-0.5
            )
            scores = jnp.where(allowed, scores, -jnp.inf)
            sink = sinks[h]
            peak = jnp.maximum(jnp.max(scores, axis=1, keepdims=True), sink)
            raised = jnp.exp(scores - peak)
            total = jnp.sum(raised, axis=1, keepdims=True) + jnp.exp(sink - peak)
            weights = (raised / total).astype(BF)
            mixed.append(jnp.dot(weights, values, preferred_element_type=F32).astype(BF))
        attended[at : at + WINDOW, :] = jnp.concatenate(mixed, axis=1)

    def project(half):
        rows_in = attended[half * half_rows : (half + 1) * half_rows, :]
        for start in range(0, width, 512):
            stop = min(start + 512, width)
            partial_rows[half, :, :, start:stop] = (
                lax.dot_general(
                    rows_in, out_weight[start:stop, :], NT, preferred_element_type=F32
                )
                .astype(BF)
                .reshape(GROUP, piece, stop - start)
            )

    policy_ag = [Gather(pool, place, policy_rows.at[h], h) for h in range(HALVES)]
    normed_ag = [Gather(pool, place, normed_rows.at[h], h) for h in range(HALVES)]

    def scatter(x, bufs, h):
        return Scatter(pool, place, x.at[h], *(buf.at[h] for buf in bufs))

    p_bufs = (p_tp, p_tm, p_fp, p_fm, p_y, p_fa)
    g_bufs = (g_tp, g_tm, g_fp, g_fm, g_y, g_fa)
    partial_rs = [scatter(partial_rows, p_bufs, h) for h in range(HALVES)]
    grad_rs = [scatter(grad_parts, g_bufs, h) for h in range(HALVES)]

    def join(land, h):
        return jnp.concatenate([land[v, h] for v in range(GROUP)], axis=1)

    def normalise(h):
        projected = partial_rs[h].result() + bias[...].reshape(1, width)
        hidden = (residual_own[h].astype(F32) + projected).astype(BF)
        wide = hidden.astype(F32)
        spread_of = jnp.sum(wide * wide, axis=1, keepdims=True) * (1.0 / width)
        normed_rows[h, own] = (wide * lax.rsqrt(spread_of + 1e-05) * gain[...].reshape(1, width)).astype(BF)

    def logits(rows_of, head, out, h, tile, tiles=3):
        cols = slice(tile * (vocab_here // tiles), (tile + 1) * (vocab_here // tiles))
        lhs = rows_of[h].reshape(half_rows, width)
        out[h, :, cols] = jnp.dot(lhs, head[:, cols], preferred_element_type=F32)

    def policy_stats(h):
        top = jnp.max(policy_logits[h], axis=1, keepdims=True)
        pol_max[h] = jnp.broadcast_to(top, pol_max.shape[1:])
        pol_sum[h] = jnp.broadcast_to(
            jnp.sum(jnp.exp(policy_logits[h] - top), axis=1, keepdims=True), pol_sum.shape[1:]
        )

    def stat_copy(h, t):
        to = lax.rem(me + t, GROUP)
        return pltpu.make_async_remote_copy(
            src_ref=stats.at[h, me],
            dst_ref=stats.at[h, me],
            send_sem=stat_sems.at[h, 0, t - 1],
            recv_sem=stat_sems.at[h, 1, t - 1],
            device_id=(place.ctx, to),
            device_id_type=MESH,
        )

    def send_stats(h):
        top = jnp.max(ref_logits[h], axis=1, keepdims=True)
        total = jnp.sum(jnp.exp(ref_logits[h] - top), axis=1, keepdims=True)
        pol_top = pol_max[h][:, :1]
        gap = jnp.sum(
            jnp.exp(policy_logits[h] - pol_top) * (policy_logits[h] - ref_logits[h]),
            axis=1,
            keepdims=True,
        )
        lane = lax.broadcasted_iota(jnp.int32, (half_rows, 128), 1)
        packed = jnp.where(lane == 0, pol_max[h], pol_sum[h])
        packed = jnp.where(lane == 2, top, packed)
        packed = jnp.where(lane == 3, total, packed)
        packed = jnp.where(lane == 4, gap, packed)
        stats[h, me] = packed.T[:8, :]
        each_peer(lambda t: stat_copy(h, t).start())

    def loss_gradient(h):
        each_peer(lambda t: stat_copy(h, t).wait_recv())
        pol_tops, pol_sums = stats[h, :, 0, :], stats[h, :, 1, :]
        ref_tops, ref_sums = stats[h, :, 2, :], stats[h, :, 3, :]
        pol_top = jnp.max(pol_tops, axis=0, keepdims=True)
        ref_top = jnp.max(ref_tops, axis=0, keepdims=True)
        scale = jnp.exp(pol_tops - pol_top)
        pol_total = jnp.sum(pol_sums * scale, axis=0, keepdims=True)
        gap = jnp.sum(stats[h, :, 4, :] * scale, axis=0, keepdims=True) / pol_total
        ref_total = jnp.sum(ref_sums * jnp.exp(ref_tops - ref_top), axis=0, keepdims=True)
        log_pol = pol_top + jnp.log(pol_total)
        log_ref = ref_top + jnp.log(ref_total)
        divergence = gap - log_pol + log_ref
        for part in range(half_rows // 128):
            lanes = slice(part * 128, (part + 1) * 128)
            at = h * (half_rows // 128) + part
            here = slice(part * 128, (part + 1) * 128)
            divergence_out[at : at + 1, :] = divergence[:, lanes]
            adv_row = advantages[at : at + 1, :]
            log_col = column(log_pol[:, lanes])
            add_col = column(adv_row - gap[:, lanes])
            adv_col = column(adv_row)
            tok_col = column(
                (token_ids[at : at + 1, :] - me * vocab_here).astype(F32)
            )
            for chunk in range(0, vocab_here, 128):
                cols = slice(chunk, chunk + 128)
                ids = (lax.broadcasted_iota(jnp.int32, (128, 128), 1) + chunk).astype(F32)
                pol = policy_logits[h, here, cols]
                prob = jnp.exp(pol - log_col)
                value = prob * (pol - ref_logits[h, here, cols] + add_col)
                logit_grad[h, here, cols] = (
                    value - jnp.where(ids == tok_col, adv_col, 0.0)
                ).astype(BF)

    def gradient(h, db):
        at = pl.ds(SIDE * place.along_b(db), SIDE)
        block_rows = head_blocks.shape[1]
        lhs = head_blocks[at].reshape(SIDE * block_rows, vocab_here)
        grad_parts[h, at] = (
            lax.dot_general(lhs, logit_grad[h], NT, preferred_element_type=F32)
            .astype(BF)
            .reshape(SIDE, block_rows, half_rows)
        )

    def finish(h):
        grad_out[:, h * half_rows : (h + 1) * half_rows] = grad_rs[h].result()[:share, :]

    one, two = 1, 0
    l_query.wait()
    attend(2)
    l_residual.wait()
    turn_over(residual_turned, residual, land_residual)
    each_peer(lambda t: spread(residual, land_residual, residual_sems, t).start())
    attend(3)
    l_out.wait()
    project(one)
    partial_rs[one].far()
    each_peer(lambda t: spread(policy_hidden, land_policy, policy_sems, t).wait_recv())
    policy_rows[one, own] = join(land_policy, one)
    partial_rs[one].near_down()
    partial_rs[one].near_up()
    policy_rows[two, own] = join(land_policy, two)
    policy_ag[one].s0()
    partial_rs[one].pass_down()
    partial_rs[one].pass_up()
    halo.wait_recv()
    attend(1)
    attend(0)
    policy_ag[one].s1()
    policy_ag[one].s2()
    l_policy_head.wait()
    for d in range(GROUP):
        head_blocks[place.block_of(d), :share, :] = policy_head[d * share : (d + 1) * share, :]
    project(two)
    policy_ag[two].s0()
    each_peer(lambda t: spread(residual, land_residual, residual_sems, t).wait_recv())
    residual_own[two] = join(land_residual, two)
    residual_own[one] = join(land_residual, one)
    partial_rs[one].turn()
    partial_rs[two].near_up()
    policy_ag[one].s4()
    partial_rs[two].far()
    policy_ag[one].s6()
    policy_ag[one].s3()
    partial_rs[two].near_down()
    normalise(one)
    normed_ag[one].s0()
    partial_rs[two].pass_up()
    policy_ag[one].s7()
    policy_ag[one].s5()
    normed_ag[one].s4()
    partial_rs[two].pass_down()
    normed_ag[one].s2()
    policy_ag[one].s8()
    policy_ag[two].s1()
    normed_ag[one].s1()
    logits(policy_rows, policy_head, policy_logits, one, 0)
    normed_ag[one].s3()
    partial_rs[two].turn()
    policy_ag[two].s3()
    logits(policy_rows, policy_head, policy_logits, one, 1)
    normed_ag[one].s5()
    normed_ag[one].s6()
    logits(policy_rows, policy_head, policy_logits, one, 2)
    policy_ag[two].s4()
    normed_ag[one].s7()
    normalise(two)
    normed_ag[two].s0()
    policy_stats(one)
    policy_ag[two].s2()
    policy_ag[two].s7()
    normed_ag[one].s8()
    l_ref_head.wait()
    logits(normed_rows, ref_head, ref_logits, one, 0)
    policy_ag[two].s5()
    logits(normed_rows, ref_head, ref_logits, one, 1)
    normed_ag[two].s1()
    logits(normed_rows, ref_head, ref_logits, one, 2)
    policy_ag[two].s6()
    send_stats(one)
    normed_ag[two].s5()
    normed_ag[two].s4()
    policy_ag[two].s8()
    normed_ag[two].s3()
    logits(policy_rows, policy_head, policy_logits, two, 0)
    normed_ag[two].s2()
    logits(policy_rows, policy_head, policy_logits, two, 1)
    logits(policy_rows, policy_head, policy_logits, two, 2)
    normed_ag[two].s6()
    normed_ag[two].s7()
    loss_gradient(one)
    gradient(one, 2)
    grad_rs[one].far()
    normed_ag[two].s8()
    gradient(one, 1)
    policy_stats(two)
    grad_rs[one].near_up()
    logits(normed_rows, ref_head, ref_logits, two, 0)
    logits(normed_rows, ref_head, ref_logits, two, 1)
    logits(normed_rows, ref_head, ref_logits, two, 2)
    send_stats(two)
    gradient(one, -1)
    grad_rs[one].near_down()
    grad_rs[one].pass_down()
    grad_rs[one].pass_up()
    loss_gradient(two)
    gradient(two, 2)
    grad_rs[two].far()
    gradient(two, 1)
    gradient(two, -1)
    grad_rs[two].near_up()
    grad_rs[two].near_down()
    grad_rs[two].pass_up()
    grad_rs[two].pass_down()
    gradient(one, 0)
    gradient(two, 0)
    grad_rs[one].turn()
    grad_rs[two].turn()
    finish(one)
    finish(two)

    for copy in pool.copies:
        copy.wait_send()
    each_peer(lambda t: spread(policy_hidden, land_policy, policy_sems, t).wait_send())
    each_peer(lambda t: spread(residual, land_residual, residual_sems, t).wait_send())
    for h in range(HALVES):
        each_peer(lambda t: stat_copy(h, t).wait_send())


def shards(
    queries,
    key_rows,
    value_rows,
    sink_logits,
    out_weight,
    out_bias,
    residual,
    norm_gain,
    policy_hidden,
    ref_head,
    policy_head,
    token_ids,
    advantages,
    positions,
):
    rows, heads_width = queries.shape
    share = residual.shape[1]
    width, vocab_here = ref_head.shape
    half_rows = rows // HALVES
    piece = half_rows // GROUP
    block_rows = -(-share // 16) * 16
    copies = 1 + HALVES * 2 * (15 + 9)

    def sums(block):
        return [
            pltpu.VMEM((HALVES, lead, *block), BF)
            for lead in (2, 2, SIDE, SIDE, SIDE - 1, SIDE - 1)
        ]

    vmem, hbm = (pl.BlockSpec(memory_space=space) for space in (pltpu.VMEM, pl.ANY))
    smem = pl.BlockSpec(memory_space=pltpu.SMEM)
    divergence, grad = pl.pallas_call(
        kernel,
        out_shape=(
            jax.ShapeDtypeStruct((rows // 128, 128), F32),
            jax.ShapeDtypeStruct((share, rows), F32),
        ),
        in_specs=[
            hbm, hbm, hbm, smem, hbm, vmem, hbm, vmem, hbm, hbm, hbm, vmem, vmem, vmem,
        ],
        out_specs=(vmem, vmem),
        scratch_shapes=[
            pltpu.VMEM((width, heads_width), BF),
            pltpu.VMEM((width, vocab_here), BF),
            pltpu.VMEM((width, vocab_here), BF),
            pltpu.VMEM((GROUP, block_rows, vocab_here), BF),
            pltpu.VMEM((rows, heads_width), BF),
            pltpu.VMEM((rows, 2 * HEAD_DIM), BF),
            pltpu.VMEM((rows, 2 * HEAD_DIM), BF),
            pltpu.VMEM((share, rows), BF),
            pltpu.VMEM((share, rows), BF),
            pltpu.VMEM((HALVES, half_rows, share), BF),
            pltpu.VMEM((HALVES, half_rows, share), BF),
            pltpu.VMEM((WINDOW + rows, 2 * HEAD_DIM), BF),
            pltpu.VMEM((rows, heads_width), BF),
            pltpu.VMEM((GROUP, HALVES, piece, share), BF),
            pltpu.VMEM((GROUP, HALVES, piece, share), BF),
            pltpu.VMEM((HALVES, piece, width), BF),
            pltpu.VMEM((HALVES, GROUP, piece, width), BF),
            pltpu.VMEM((HALVES, GROUP, piece, width), BF),
            pltpu.VMEM((HALVES, GROUP, piece, width), BF),
            pltpu.VMEM((HALVES, half_rows, vocab_here), F32),
            pltpu.VMEM((HALVES, half_rows, vocab_here), F32),
            pltpu.VMEM((HALVES, half_rows, vocab_here), BF),
            pltpu.VMEM((HALVES, GROUP, block_rows, half_rows), BF),
            pltpu.VMEM((HALVES, half_rows, 128), F32),
            pltpu.VMEM((HALVES, half_rows, 128), F32),
            pltpu.VMEM((HALVES, GROUP, 8, half_rows), F32),
            *sums((piece, width)),
            *sums((block_rows, half_rows)),
            pltpu.SemaphoreType.DMA((8,)),
            pltpu.SemaphoreType.DMA((copies,)),
            pltpu.SemaphoreType.DMA((copies,)),
            pltpu.SemaphoreType.DMA((2, GROUP - 1)),
            pltpu.SemaphoreType.DMA((2, GROUP - 1)),
            pltpu.SemaphoreType.DMA((HALVES, 2, GROUP - 1)),
        ],
        compiler_params=pltpu.CompilerParams(
            collective_id=0, has_side_effects=True, vmem_limit_bytes=62 << 20
        ),
    )(
        queries,
        key_rows,
        value_rows,
        sink_logits,
        out_weight.T,
        out_bias,
        residual.T,
        norm_gain,
        policy_hidden.T,
        ref_head,
        policy_head,
        token_ids.reshape(rows // 128, 128),
        advantages.reshape(rows // 128, 128),
        positions.reshape(rows // 128, 128),
    )
    return divergence.reshape(rows), grad


def solution(mesh):
    return jax.shard_map(
        shards,
        mesh=mesh,
        in_specs=(
            P("ctx", "vocab"),
            P("ctx", None),
            P("ctx", None),
            P("vocab"),
            P("vocab", None),
            P(),
            P("ctx", "vocab"),
            P(),
            P("ctx", "vocab"),
            P(None, "vocab"),
            P(None, "vocab"),
            P("ctx"),
            P("ctx"),
            P("ctx"),
        ),
        out_specs=(P("ctx"), P("vocab", "ctx")),
        check_vma=False,
    )
```

```python
import functools

import jax
import jax.numpy as jnp
from jax import lax
from jax.experimental import pallas as pl
from jax.experimental.pallas import tpu as pltpu
from jax.sharding import PartitionSpec as P

MESH = pl.DeviceIdType.MESH
BF = jnp.bfloat16
F32 = jnp.float32
HEAD_DIM = 64
WINDOW = 128
SIDE = 4
GROUP = SIDE * SIDE
HALVES = 2
NT = (((1,), (1,)), ((), ()))


class Pool:
    def __init__(self, send_sems, recv_sems):
        self.send_sems, self.recv_sems = send_sems, recv_sems
        self.copies = []

    def start(self, src, dst, device):
        at = len(self.copies)
        copy = pltpu.make_async_remote_copy(
            src_ref=src,
            dst_ref=dst,
            send_sem=self.send_sems.at[at],
            recv_sem=self.recv_sems.at[at],
            device_id=device,
            device_id_type=MESH,
        )
        copy.start()
        self.copies.append(copy)
        return copy


def add_into(dst, src):
    dst[...] = (dst[...].astype(F32) + src[...].astype(F32)).astype(BF)


class Gather:
    def __init__(self, pool, place, buf, half):
        self.pool, self.place, self.buf, self.half = pool, place, buf, half

    def piece(self, da, db):
        return self.buf.at[self.place.block(da, db)]

    def send(self, piece, da, db):
        return self.pool.start(piece, piece, self.place.device(da, db))

    def s0(self):
        own = self.piece(0, 0)
        self.ap, self.am = self.send(own, 1, 0), self.send(own, -1, 0)
        self.bp0, self.bm0 = self.send(own, 0, 1), self.send(own, 0, -1)

    def s1(self):
        self.ap.wait_recv()
        got = self.piece(-1, 0)
        if self.half == 0:
            self.a2 = self.send(got, 1, 0)
        self.bp1, self.bm1 = self.send(got, 0, 1), self.send(got, 0, -1)

    def s2(self):
        self.am.wait_recv()
        got = self.piece(1, 0)
        if self.half == 1:
            self.a2 = self.send(got, -1, 0)
        self.bp2, self.bm2 = self.send(got, 0, 1), self.send(got, 0, -1)

    def s3(self):
        self.a2.wait_recv()
        got = self.piece(2, 0)
        self.bp3, self.bm3 = self.send(got, 0, 1), self.send(got, 0, -1)

    def s4(self):
        self.bp0.wait_recv()
        self.f0 = self.send(self.piece(0, -1), 0, 1)

    def s5(self):
        self.bp1.wait_recv()
        self.f1 = self.send(self.piece(-1, -1), 0, 1)

    def s6(self):
        self.bm2.wait_recv()
        self.f2 = self.send(self.piece(1, 1), 0, -1)

    def s7(self):
        self.bm3.wait_recv()
        self.f3 = self.send(self.piece(2, 1), 0, -1)

    def s8(self):
        for copy in (self.bm0, self.bm1, self.bp2, self.bp3, self.f0, self.f1, self.f2, self.f3):
            copy.wait_recv()


class Scatter:
    def __init__(self, pool, place, x, tp, tm, fp, fm, y, fa):
        self.pool, self.place = pool, place
        self.x, self.tp, self.tm, self.fp, self.fm = x, tp, tm, fp, fm
        self.y, self.fa = y, fa

    def group(self, db, first, count):
        return self.x.at[pl.ds(SIDE * self.place.along_b(db) + first, count)]

    def send(self, src, dst, db):
        return self.pool.start(src, dst, self.place.device(0, db))

    def far(self):
        self.c_tp = self.send(self.group(2, 0, 2), self.tp, 1)
        self.c_tm = self.send(self.group(2, 2, 2), self.tm, -1)

    def near_up(self):
        self.c_fp2 = self.send(self.group(1, 2, 2), self.fp.at[pl.ds(2, 2)], 1)

    def near_down(self):
        self.c_fm0 = self.send(self.group(-1, 0, 2), self.fm.at[pl.ds(0, 2)], -1)

    def pass_up(self):
        self.c_tp.wait_recv()
        add_into(self.group(1, 0, 2), self.tp)
        self.c_fp0 = self.send(self.group(1, 0, 2), self.fp.at[pl.ds(0, 2)], 1)

    def pass_down(self):
        self.c_tm.wait_recv()
        add_into(self.group(-1, 2, 2), self.tm)
        self.c_fm2 = self.send(self.group(-1, 2, 2), self.fm.at[pl.ds(2, 2)], -1)

    def here(self, i):
        return (
            self.x[SIDE * self.place.b + i].astype(F32)
            + self.fp[i].astype(F32)
            + self.fm[i].astype(F32)
        )

    def turn(self):
        for copy in (self.c_fp2, self.c_fm0, self.c_fp0, self.c_fm2):
            copy.wait_recv()
        self.c_fa = []
        for slot, da in enumerate((2, 1, -1)):
            to = self.place.along_a(da)
            self.y[slot] = self.here(to).astype(BF)
            self.c_fa.append(
                self.pool.start(self.y.at[slot], self.fa.at[slot], self.place.device(da, 0))
            )

    def result(self):
        total = self.here(self.place.a)
        for slot in range(SIDE - 1):
            self.c_fa[slot].wait_recv()
            total = total + self.fa[slot].astype(F32)
        return total


class Place:
    def __init__(self):
        self.ctx, self.vocab = lax.axis_index("ctx"), lax.axis_index("vocab")
        self.z, self.x = self.vocab // SIDE, lax.rem(self.vocab, SIDE)
        self.core = lax.rem(self.ctx, 2)
        self.a = self.x * (1 - self.core) + self.z * self.core
        self.b = self.z * (1 - self.core) + self.x * self.core

    def along_a(self, da):
        return lax.rem(self.a + (da + SIDE), SIDE)

    def along_b(self, db):
        return lax.rem(self.b + (db + SIDE), SIDE)

    def block(self, da, db):
        return SIDE * self.along_b(db) + self.along_a(da)

    def device(self, da, db):
        a, b = self.along_a(da), self.along_b(db)
        return (self.ctx, a * (1 + 3 * self.core) + b * (4 - 3 * self.core))

    def block_of(self, vocab):
        turned = SIDE * lax.rem(vocab, SIDE) + vocab // SIDE
        return vocab * (1 - self.core) + turned * self.core


def column(row):
    return jnp.broadcast_to(row, (128, 128)).T


def kernel(
    queries_hbm,
    key_rows_hbm,
    value_rows_hbm,
    sinks,
    out_weight_hbm,
    bias,
    residual_hbm,
    gain,
    policy_hidden_hbm,
    ref_head_hbm,
    policy_head_hbm,
    token_ids,
    advantages,
    positions,
    divergence_out,
    grad_out,
    out_weight,
    ref_head,
    policy_head,
    head_blocks,
    queries,
    key_pair,
    value_pair,
    policy_turned,
    residual_turned,
    policy_hidden,
    residual,
    kv,
    attended,
    land_policy,
    land_residual,
    residual_own,
    policy_rows,
    normed_rows,
    partial_rows,
    policy_logits,
    ref_logits,
    logit_grad,
    grad_parts,
    pol_max,
    pol_sum,
    stats,
    p_tp,
    p_tm,
    p_fp,
    p_fm,
    p_y,
    p_fa,
    g_tp,
    g_tm,
    g_fp,
    g_fm,
    g_y,
    g_fa,
    local_sems,
    send_sems,
    recv_sems,
    policy_sems,
    residual_sems,
    stat_sems,
):
    rows, width = attended.shape[0], out_weight.shape[0]
    half_rows = rows // HALVES
    piece = half_rows // GROUP
    share = land_policy.shape[3]
    vocab_here = ref_head.shape[1]
    place = Place()
    me = place.vocab
    own = place.block(0, 0)

    kv_lanes = pl.ds(pl.multiple_of(place.z * 128, 128), 128)
    loads = [
        pltpu.make_async_copy(src, dst, local_sems.at[i])
        for i, (src, dst) in enumerate(
            (
                (policy_hidden_hbm, policy_turned),
                (key_rows_hbm.at[:, kv_lanes], key_pair),
                (value_rows_hbm.at[:, kv_lanes], value_pair),
                (queries_hbm, queries),
                (out_weight_hbm, out_weight),
                (residual_hbm, residual_turned),
                (policy_head_hbm, policy_head),
                (ref_head_hbm, ref_head),
            )
        )
    ]
    l_policy, l_key, l_value, l_query, l_out, l_residual, l_policy_head, l_ref_head = loads
    for load in loads:
        load.start()

    barrier = pltpu.get_barrier_semaphore()
    ctx_count = lax.axis_size("ctx")
    next_ctx = lax.rem(place.ctx + 1, ctx_count)
    last_ctx = lax.rem(place.ctx + ctx_count - 1, ctx_count)
    for other in (next_ctx, last_ctx):
        pl.semaphore_signal(barrier, inc=1, device_id=(other, me), device_id_type=MESH)

    def greet(t, carry):
        pl.semaphore_signal(
            barrier,
            inc=1,
            device_id=(place.ctx, lax.rem(me + t, GROUP)),
            device_id_type=MESH,
        )
        return carry

    lax.fori_loop(1, GROUP, greet, 0)

    own_rows = pl.ds(pl.multiple_of(own * piece, piece), piece)

    def turn_over(source, out, land):
        for h in range(HALVES):
            out[h] = source[:, h * half_rows : (h + 1) * half_rows].T
        land[me] = out[:, own_rows, :]

    l_policy.wait()
    turn_over(policy_turned, policy_hidden, land_policy)

    upper = lax.rem(me // 2, 2) == 1
    l_key.wait()
    l_value.wait()
    for pair, lane in ((key_pair, 0), (value_pair, HEAD_DIM)):
        kv[pl.ds(WINDOW, rows), lane : lane + HEAD_DIM] = jnp.where(
            upper, pair[:, HEAD_DIM:], pair[:, :HEAD_DIM]
        )

    pl.semaphore_wait(barrier, GROUP - 1 + 2)

    pool = Pool(send_sems, recv_sems)
    halo = pool.start(kv.at[pl.ds(rows, WINDOW)], kv.at[pl.ds(0, WINDOW)], (next_ctx, me))

    def spread(source, land, sems, t):
        to = lax.rem(me + t, GROUP)
        block = pl.ds(pl.multiple_of(place.block_of(to) * piece, piece), piece)
        return pltpu.make_async_remote_copy(
            src_ref=source.at[:, block, :],
            dst_ref=land.at[me],
            send_sem=sems.at[0, t - 1],
            recv_sem=sems.at[1, t - 1],
            device_id=(place.ctx, to),
            device_id_type=MESH,
        )

    def each_peer(act):
        def body(t, carry):
            act(t)
            return carry

        lax.fori_loop(1, GROUP, body, 0)

    each_peer(lambda t: spread(policy_hidden, land_policy, policy_sems, t).start())
    l_residual.wait()
    turn_over(residual_turned, residual, land_residual)
    each_peer(lambda t: spread(residual, land_residual, residual_sems, t).start())

    def attend(block):
        at = block * WINDOW
        keys = kv[at : at + 2 * WINDOW, :HEAD_DIM]
        values = kv[at : at + 2 * WINDOW, HEAD_DIM:]
        query = queries[at : at + WINDOW, :]
        heads = query.shape[1] // HEAD_DIM
        offsets = (
            lax.broadcasted_iota(jnp.int32, (WINDOW, 2 * WINDOW), 0)
            + WINDOW
            - lax.broadcasted_iota(jnp.int32, (WINDOW, 2 * WINDOW), 1)
        )
        where_at = column(positions[block : block + 1, :].astype(F32))
        where_at = jnp.concatenate([where_at, where_at], axis=1)
        allowed = (offsets >= 0) & (offsets < WINDOW) & (where_at >= offsets.astype(F32))
        mixed = []
        for h in range(heads):
            scores = (
                lax.dot_general(
                    query[:, h * HEAD_DIM : (h + 1) * HEAD_DIM],
                    keys,
                    NT,
                    preferred_element_type=F32,
                )
                * HEAD_DIM**-0.5
            )
            scores = jnp.where(allowed, scores, -jnp.inf)
            sink = sinks[h]
            peak = jnp.maximum(jnp.max(scores, axis=1, keepdims=True), sink)
            raised = jnp.exp(scores - peak)
            total = jnp.sum(raised, axis=1, keepdims=True) + jnp.exp(sink - peak)
            weights = (raised / total).astype(BF)
            mixed.append(jnp.dot(weights, values, preferred_element_type=F32).astype(BF))
        attended[at : at + WINDOW, :] = jnp.concatenate(mixed, axis=1)

    def project(half):
        rows_in = attended[half * half_rows : (half + 1) * half_rows, :]
        for start in range(0, width, 512):
            stop = min(start + 512, width)
            partial_rows[half, :, :, start:stop] = (
                lax.dot_general(
                    rows_in, out_weight[start:stop, :], NT, preferred_element_type=F32
                )
                .astype(BF)
                .reshape(GROUP, piece, stop - start)
            )

    policy_ag = [Gather(pool, place, policy_rows.at[h], h) for h in range(HALVES)]
    normed_ag = [Gather(pool, place, normed_rows.at[h], h) for h in range(HALVES)]

    def scatter(x, bufs, h):
        return Scatter(pool, place, x.at[h], *(buf.at[h] for buf in bufs))

    p_bufs = (p_tp, p_tm, p_fp, p_fm, p_y, p_fa)
    g_bufs = (g_tp, g_tm, g_fp, g_fm, g_y, g_fa)
    partial_rs = [scatter(partial_rows, p_bufs, h) for h in range(HALVES)]
    grad_rs = [scatter(grad_parts, g_bufs, h) for h in range(HALVES)]

    def join(land, h):
        return jnp.concatenate([land[v, h] for v in range(GROUP)], axis=1)

    def normalise(h):
        projected = partial_rs[h].result() + bias[...].reshape(1, width)
        hidden = (residual_own[h].astype(F32) + projected).astype(BF)
        wide = hidden.astype(F32)
        spread_of = jnp.sum(wide * wide, axis=1, keepdims=True) * (1.0 / width)
        normed_rows[h, own] = (wide * lax.rsqrt(spread_of + 1e-05) * gain[...].reshape(1, width)).astype(BF)

    def logits(rows_of, head, out, h, tile, tiles=3):
        cols = slice(tile * (vocab_here // tiles), (tile + 1) * (vocab_here // tiles))
        lhs = rows_of[h].reshape(half_rows, width)
        out[h, :, cols] = jnp.dot(lhs, head[:, cols], preferred_element_type=F32)

    def policy_stats(h):
        top = jnp.max(policy_logits[h], axis=1, keepdims=True)
        pol_max[h] = jnp.broadcast_to(top, pol_max.shape[1:])
        pol_sum[h] = jnp.broadcast_to(
            jnp.sum(jnp.exp(policy_logits[h] - top), axis=1, keepdims=True), pol_sum.shape[1:]
        )

    def stat_copy(h, t):
        to = lax.rem(me + t, GROUP)
        return pltpu.make_async_remote_copy(
            src_ref=stats.at[h, me],
            dst_ref=stats.at[h, me],
            send_sem=stat_sems.at[h, 0, t - 1],
            recv_sem=stat_sems.at[h, 1, t - 1],
            device_id=(place.ctx, to),
            device_id_type=MESH,
        )

    def send_stats(h):
        top = jnp.max(ref_logits[h], axis=1, keepdims=True)
        total = jnp.sum(jnp.exp(ref_logits[h] - top), axis=1, keepdims=True)
        pol_top = pol_max[h][:, :1]
        gap = jnp.sum(
            jnp.exp(policy_logits[h] - pol_top) * (policy_logits[h] - ref_logits[h]),
            axis=1,
            keepdims=True,
        )
        lane = lax.broadcasted_iota(jnp.int32, (half_rows, 128), 1)
        packed = jnp.where(lane == 0, pol_max[h], pol_sum[h])
        packed = jnp.where(lane == 2, top, packed)
        packed = jnp.where(lane == 3, total, packed)
        packed = jnp.where(lane == 4, gap, packed)
        stats[h, me] = packed.T[:8, :]
        each_peer(lambda t: stat_copy(h, t).start())

    def loss_gradient(h):
        each_peer(lambda t: stat_copy(h, t).wait_recv())
        pol_tops, pol_sums = stats[h, :, 0, :], stats[h, :, 1, :]
        ref_tops, ref_sums = stats[h, :, 2, :], stats[h, :, 3, :]
        pol_top = jnp.max(pol_tops, axis=0, keepdims=True)
        ref_top = jnp.max(ref_tops, axis=0, keepdims=True)
        scale = jnp.exp(pol_tops - pol_top)
        pol_total = jnp.sum(pol_sums * scale, axis=0, keepdims=True)
        gap = jnp.sum(stats[h, :, 4, :] * scale, axis=0, keepdims=True) / pol_total
        ref_total = jnp.sum(ref_sums * jnp.exp(ref_tops - ref_top), axis=0, keepdims=True)
        log_pol = pol_top + jnp.log(pol_total)
        log_ref = ref_top + jnp.log(ref_total)
        divergence = gap - log_pol + log_ref
        for part in range(half_rows // 128):
            lanes = slice(part * 128, (part + 1) * 128)
            at = h * (half_rows // 128) + part
            here = slice(part * 128, (part + 1) * 128)
            divergence_out[at : at + 1, :] = divergence[:, lanes]
            adv_row = advantages[at : at + 1, :]
            log_col = column(log_pol[:, lanes])
            add_col = column(adv_row - gap[:, lanes])
            adv_col = column(adv_row)
            tok_col = column(
                (token_ids[at : at + 1, :] - me * vocab_here).astype(F32)
            )
            for chunk in range(0, vocab_here, 128):
                cols = slice(chunk, chunk + 128)
                ids = (lax.broadcasted_iota(jnp.int32, (128, 128), 1) + chunk).astype(F32)
                pol = policy_logits[h, here, cols]
                prob = jnp.exp(pol - log_col)
                value = prob * (pol - ref_logits[h, here, cols] + add_col)
                logit_grad[h, here, cols] = (
                    value - jnp.where(ids == tok_col, adv_col, 0.0)
                ).astype(BF)

    def gradient(h, db):
        at = pl.ds(SIDE * place.along_b(db), SIDE)
        block_rows = head_blocks.shape[1]
        lhs = head_blocks[at].reshape(SIDE * block_rows, vocab_here)
        grad_parts[h, at] = (
            lax.dot_general(lhs, logit_grad[h], NT, preferred_element_type=F32)
            .astype(BF)
            .reshape(SIDE, block_rows, half_rows)
        )

    def finish(h):
        grad_out[:, h * half_rows : (h + 1) * half_rows] = grad_rs[h].result()[:share, :]

    one, two = 1, 0
    l_query.wait()
    attend(3)
    attend(2)
    l_out.wait()
    project(one)
    partial_rs[one].far()
    partial_rs[one].near_down()
    halo.wait_recv()
    attend(1)
    partial_rs[one].near_up()
    attend(0)
    project(two)
    partial_rs[two].near_down()
    each_peer(lambda t: spread(policy_hidden, land_policy, policy_sems, t).wait_recv())
    policy_rows[one, own] = join(land_policy, one)
    policy_ag[one].s0()
    partial_rs[one].pass_down()
    each_peer(lambda t: spread(residual, land_residual, residual_sems, t).wait_recv())
    residual_own[one] = join(land_residual, one)
    partial_rs[two].far()
    partial_rs[one].pass_up()
    residual_own[two] = join(land_residual, two)
    partial_rs[two].near_up()
    policy_rows[two, own] = join(land_policy, two)
    policy_ag[one].s2()
    policy_ag[two].s0()
    partial_rs[one].turn()
    partial_rs[two].pass_down()
    partial_rs[two].pass_up()
    policy_ag[two].s2()
    policy_ag[one].s3()
    normalise(one)
    policy_ag[one].s1()
    normed_ag[one].s0()
    partial_rs[two].turn()
    policy_ag[one].s4()
    policy_ag[two].s1()
    normed_ag[one].s2()
    normed_ag[one].s1()
    normed_ag[one].s3()
    normed_ag[one].s4()
    normalise(two)
    policy_ag[one].s6()
    policy_ag[one].s5()
    l_policy_head.wait()
    for d in range(GROUP):
        head_blocks[place.block_of(d), :share, :] = policy_head[d * share : (d + 1) * share, :]
    policy_ag[one].s7()
    normed_ag[two].s0()
    normed_ag[one].s6()
    normed_ag[one].s5()
    normed_ag[one].s7()
    policy_ag[one].s8()
    normed_ag[two].s1()
    logits(policy_rows, policy_head, policy_logits, one, 0)
    policy_ag[two].s5()
    policy_ag[two].s3()
    logits(policy_rows, policy_head, policy_logits, one, 1)
    logits(policy_rows, policy_head, policy_logits, one, 2)
    policy_ag[two].s4()
    normed_ag[one].s8()
    normed_ag[two].s3()
    policy_ag[two].s6()
    policy_stats(one)
    l_ref_head.wait()
    logits(normed_rows, ref_head, ref_logits, one, 0)
    normed_ag[two].s2()
    policy_ag[two].s7()
    logits(normed_rows, ref_head, ref_logits, one, 1)
    normed_ag[two].s7()
    logits(normed_rows, ref_head, ref_logits, one, 2)
    normed_ag[two].s5()
    send_stats(one)
    normed_ag[two].s4()
    normed_ag[two].s6()
    policy_ag[two].s8()
    logits(policy_rows, policy_head, policy_logits, two, 0)
    logits(policy_rows, policy_head, policy_logits, two, 1)
    logits(policy_rows, policy_head, policy_logits, two, 2)
    policy_stats(two)
    normed_ag[two].s8()
    logits(normed_rows, ref_head, ref_logits, two, 0)
    logits(normed_rows, ref_head, ref_logits, two, 1)
    logits(normed_rows, ref_head, ref_logits, two, 2)
    send_stats(two)
    loss_gradient(one)
    gradient(one, 2)
    grad_rs[one].far()
    gradient(one, 1)
    gradient(one, -1)
    grad_rs[one].near_up()
    grad_rs[one].near_down()
    grad_rs[one].pass_up()
    grad_rs[one].pass_down()
    gradient(one, 0)
    loss_gradient(two)
    gradient(two, 2)
    grad_rs[two].far()
    gradient(two, 1)
    grad_rs[two].near_up()
    gradient(two, -1)
    gradient(two, 0)
    grad_rs[two].near_down()
    grad_rs[two].pass_up()
    grad_rs[two].pass_down()
    grad_rs[one].turn()
    grad_rs[two].turn()
    finish(one)
    finish(two)

    for copy in pool.copies:
        copy.wait_send()
    each_peer(lambda t: spread(policy_hidden, land_policy, policy_sems, t).wait_send())
    each_peer(lambda t: spread(residual, land_residual, residual_sems, t).wait_send())
    for h in range(HALVES):
        each_peer(lambda t: stat_copy(h, t).wait_send())


def hand_over(divergence, grad, divergence_out, grad_out):
    divergence_out[...] = divergence[...]
    grad_out[...] = grad[...]


def shards(
    queries,
    key_rows,
    value_rows,
    sink_logits,
    out_weight,
    out_bias,
    residual,
    norm_gain,
    policy_hidden,
    ref_head,
    policy_head,
    token_ids,
    advantages,
    positions,
):
    rows, heads_width = queries.shape
    share = residual.shape[1]
    width, vocab_here = ref_head.shape
    half_rows = rows // HALVES
    piece = half_rows // GROUP
    block_rows = -(-share // 16) * 16
    copies = 1 + HALVES * 2 * (15 + 9)

    def sums(block):
        return [
            pltpu.VMEM((HALVES, lead, *block), BF)
            for lead in (2, 2, SIDE, SIDE, SIDE - 1, SIDE - 1)
        ]

    vmem, hbm = (pl.BlockSpec(memory_space=space) for space in (pltpu.VMEM, pl.ANY))
    smem = pl.BlockSpec(memory_space=pltpu.SMEM)
    divergence, grad = pl.pallas_call(
        kernel,
        out_shape=(
            jax.ShapeDtypeStruct((rows // 128, 128), F32),
            jax.ShapeDtypeStruct((share, rows), F32),
        ),
        in_specs=[
            hbm, hbm, hbm, smem, hbm, vmem, hbm, vmem, hbm, hbm, hbm, vmem, vmem, vmem,
        ],
        out_specs=(vmem, vmem),
        scratch_shapes=[
            pltpu.VMEM((width, heads_width), BF),
            pltpu.VMEM((width, vocab_here), BF),
            pltpu.VMEM((width, vocab_here), BF),
            pltpu.VMEM((GROUP, block_rows, vocab_here), BF),
            pltpu.VMEM((rows, heads_width), BF),
            pltpu.VMEM((rows, 2 * HEAD_DIM), BF),
            pltpu.VMEM((rows, 2 * HEAD_DIM), BF),
            pltpu.VMEM((share, rows), BF),
            pltpu.VMEM((share, rows), BF),
            pltpu.VMEM((HALVES, half_rows, share), BF),
            pltpu.VMEM((HALVES, half_rows, share), BF),
            pltpu.VMEM((WINDOW + rows, 2 * HEAD_DIM), BF),
            pltpu.VMEM((rows, heads_width), BF),
            pltpu.VMEM((GROUP, HALVES, piece, share), BF),
            pltpu.VMEM((GROUP, HALVES, piece, share), BF),
            pltpu.VMEM((HALVES, piece, width), BF),
            pltpu.VMEM((HALVES, GROUP, piece, width), BF),
            pltpu.VMEM((HALVES, GROUP, piece, width), BF),
            pltpu.VMEM((HALVES, GROUP, piece, width), BF),
            pltpu.VMEM((HALVES, half_rows, vocab_here), F32),
            pltpu.VMEM((HALVES, half_rows, vocab_here), F32),
            pltpu.VMEM((HALVES, half_rows, vocab_here), BF),
            pltpu.VMEM((HALVES, GROUP, block_rows, half_rows), BF),
            pltpu.VMEM((HALVES, half_rows, 128), F32),
            pltpu.VMEM((HALVES, half_rows, 128), F32),
            pltpu.VMEM((HALVES, GROUP, 8, half_rows), F32),
            *sums((piece, width)),
            *sums((block_rows, half_rows)),
            pltpu.SemaphoreType.DMA((8,)),
            pltpu.SemaphoreType.DMA((copies,)),
            pltpu.SemaphoreType.DMA((copies,)),
            pltpu.SemaphoreType.DMA((2, GROUP - 1)),
            pltpu.SemaphoreType.DMA((2, GROUP - 1)),
            pltpu.SemaphoreType.DMA((HALVES, 2, GROUP - 1)),
        ],
        compiler_params=pltpu.CompilerParams(
            collective_id=0, has_side_effects=True, vmem_limit_bytes=62 << 20
        ),
    )(
        queries,
        key_rows,
        value_rows,
        sink_logits,
        out_weight.T,
        out_bias,
        residual.T,
        norm_gain,
        policy_hidden.T,
        ref_head,
        policy_head,
        token_ids.reshape(rows // 128, 128),
        advantages.reshape(rows // 128, 128),
        positions.reshape(rows // 128, 128),
    )
    divergence, grad = pl.pallas_call(
        hand_over,
        out_shape=(
            jax.ShapeDtypeStruct(divergence.shape, F32),
            jax.ShapeDtypeStruct(grad.shape, F32),
        ),
        in_specs=[vmem, vmem],
        out_specs=(vmem, vmem),
    )(divergence, grad)
    return divergence.reshape(rows), grad


def solution(mesh):
    return jax.shard_map(
        shards,
        mesh=mesh,
        in_specs=(
            P("ctx", "vocab"),
            P("ctx", None),
            P("ctx", None),
            P("vocab"),
            P("vocab", None),
            P(),
            P("ctx", "vocab"),
            P(),
            P("ctx", "vocab"),
            P(None, "vocab"),
            P(None, "vocab"),
            P("ctx"),
            P("ctx"),
            P("ctx"),
        ),
        out_specs=(P("ctx"), P("vocab", "ctx")),
        check_vma=False,
    )
```

```python
import functools

import jax
import jax.numpy as jnp
from jax import lax
from jax.experimental import pallas as pl
from jax.experimental.pallas import tpu as pltpu
from jax.sharding import PartitionSpec as P

MESH = pl.DeviceIdType.MESH
BF = jnp.bfloat16
F32 = jnp.float32
HEAD_DIM = 64
WINDOW = 128
SIDE = 4
GROUP = SIDE * SIDE
HALVES = 2
NT = (((1,), (1,)), ((), ()))


class Pool:
    def __init__(self, send_sems, recv_sems):
        self.send_sems, self.recv_sems = send_sems, recv_sems
        self.copies = []

    def start(self, src, dst, device):
        at = len(self.copies)
        copy = pltpu.make_async_remote_copy(
            src_ref=src,
            dst_ref=dst,
            send_sem=self.send_sems.at[at],
            recv_sem=self.recv_sems.at[at],
            device_id=device,
            device_id_type=MESH,
        )
        copy.start()
        self.copies.append(copy)
        return copy


def add_into(dst, src):
    dst[...] = (dst[...].astype(F32) + src[...].astype(F32)).astype(BF)


class Gather:
    def __init__(self, pool, place, buf, half):
        self.pool, self.place, self.buf, self.half = pool, place, buf, half

    def piece(self, da, db):
        return self.buf.at[self.place.block(da, db)]

    def send(self, piece, da, db):
        return self.pool.start(piece, piece, self.place.device(da, db))

    def s0(self):
        own = self.piece(0, 0)
        self.ap, self.am = self.send(own, 1, 0), self.send(own, -1, 0)
        self.bp0, self.bm0 = self.send(own, 0, 1), self.send(own, 0, -1)

    def s1(self):
        self.ap.wait_recv()
        got = self.piece(-1, 0)
        if self.half == 0:
            self.a2 = self.send(got, 1, 0)
        self.bp1, self.bm1 = self.send(got, 0, 1), self.send(got, 0, -1)

    def s2(self):
        self.am.wait_recv()
        got = self.piece(1, 0)
        if self.half == 1:
            self.a2 = self.send(got, -1, 0)
        self.bp2, self.bm2 = self.send(got, 0, 1), self.send(got, 0, -1)

    def s3(self):
        self.a2.wait_recv()
        got = self.piece(2, 0)
        self.bp3, self.bm3 = self.send(got, 0, 1), self.send(got, 0, -1)

    def s4(self):
        self.bp0.wait_recv()
        self.f0 = self.send(self.piece(0, -1), 0, 1)

    def s5(self):
        self.bp1.wait_recv()
        self.f1 = self.send(self.piece(-1, -1), 0, 1)

    def s6(self):
        self.bm2.wait_recv()
        self.f2 = self.send(self.piece(1, 1), 0, -1)

    def s7(self):
        self.bm3.wait_recv()
        self.f3 = self.send(self.piece(2, 1), 0, -1)

    def s8(self):
        for copy in (self.bm0, self.bm1, self.bp2, self.bp3, self.f0, self.f1, self.f2, self.f3):
            copy.wait_recv()


class Scatter:
    def __init__(self, pool, place, x, tp, tm, fp, fm, y, fa):
        self.pool, self.place = pool, place
        self.x, self.tp, self.tm, self.fp, self.fm = x, tp, tm, fp, fm
        self.y, self.fa = y, fa

    def group(self, db, first, count):
        return self.x.at[pl.ds(SIDE * self.place.along_b(db) + first, count)]

    def send(self, src, dst, db):
        return self.pool.start(src, dst, self.place.device(0, db))

    def far(self):
        self.c_tp = self.send(self.group(2, 0, 2), self.tp, 1)
        self.c_tm = self.send(self.group(2, 2, 2), self.tm, -1)

    def near_up(self):
        self.c_fp2 = self.send(self.group(1, 2, 2), self.fp.at[pl.ds(2, 2)], 1)

    def near_down(self):
        self.c_fm0 = self.send(self.group(-1, 0, 2), self.fm.at[pl.ds(0, 2)], -1)

    def pass_up(self):
        self.c_tp.wait_recv()
        add_into(self.group(1, 0, 2), self.tp)
        self.c_fp0 = self.send(self.group(1, 0, 2), self.fp.at[pl.ds(0, 2)], 1)

    def pass_down(self):
        self.c_tm.wait_recv()
        add_into(self.group(-1, 2, 2), self.tm)
        self.c_fm2 = self.send(self.group(-1, 2, 2), self.fm.at[pl.ds(2, 2)], -1)

    def here(self, i):
        return (
            self.x[SIDE * self.place.b + i].astype(F32)
            + self.fp[i].astype(F32)
            + self.fm[i].astype(F32)
        )

    def turn(self):
        for copy in (self.c_fp2, self.c_fm0, self.c_fp0, self.c_fm2):
            copy.wait_recv()
        self.c_fa = []
        for slot, da in enumerate((2, 1, -1)):
            to = self.place.along_a(da)
            self.y[slot] = self.here(to).astype(BF)
            self.c_fa.append(
                self.pool.start(self.y.at[slot], self.fa.at[slot], self.place.device(da, 0))
            )

    def result(self):
        total = self.here(self.place.a)
        for slot in range(SIDE - 1):
            self.c_fa[slot].wait_recv()
            total = total + self.fa[slot].astype(F32)
        return total


class Place:
    def __init__(self):
        self.ctx, self.vocab = lax.axis_index("ctx"), lax.axis_index("vocab")
        self.z, self.x = self.vocab // SIDE, lax.rem(self.vocab, SIDE)
        self.core = lax.rem(self.ctx, 2)
        self.a = self.x * (1 - self.core) + self.z * self.core
        self.b = self.z * (1 - self.core) + self.x * self.core

    def along_a(self, da):
        return lax.rem(self.a + (da + SIDE), SIDE)

    def along_b(self, db):
        return lax.rem(self.b + (db + SIDE), SIDE)

    def block(self, da, db):
        return SIDE * self.along_b(db) + self.along_a(da)

    def device(self, da, db):
        a, b = self.along_a(da), self.along_b(db)
        return (self.ctx, a * (1 + 3 * self.core) + b * (4 - 3 * self.core))

    def block_of(self, vocab):
        turned = SIDE * lax.rem(vocab, SIDE) + vocab // SIDE
        return vocab * (1 - self.core) + turned * self.core


def column(row):
    return jnp.broadcast_to(row, (128, 128)).T


def kernel(
    queries_hbm,
    key_rows_hbm,
    value_rows_hbm,
    sinks,
    out_weight_hbm,
    bias,
    residual_hbm,
    gain,
    policy_hidden_hbm,
    ref_head_hbm,
    policy_head_hbm,
    token_ids,
    advantages,
    positions,
    divergence_out,
    grad_out,
    out_weight,
    ref_head,
    policy_head,
    head_blocks,
    queries,
    key_pair,
    value_pair,
    policy_turned,
    residual_turned,
    policy_hidden,
    residual,
    kv,
    attended,
    land_policy,
    land_residual,
    residual_own,
    policy_rows,
    normed_rows,
    partial_rows,
    policy_logits,
    ref_logits,
    logit_grad,
    grad_parts,
    pol_max,
    pol_sum,
    stats,
    p_tp,
    p_tm,
    p_fp,
    p_fm,
    p_y,
    p_fa,
    g_tp,
    g_tm,
    g_fp,
    g_fm,
    g_y,
    g_fa,
    local_sems,
    send_sems,
    recv_sems,
    policy_sems,
    residual_sems,
    stat_sems,
):
    rows, width = attended.shape[0], out_weight.shape[0]
    half_rows = rows // HALVES
    piece = half_rows // GROUP
    share = land_policy.shape[3]
    vocab_here = ref_head.shape[1]
    place = Place()
    me = place.vocab
    own = place.block(0, 0)

    kv_lanes = pl.ds(pl.multiple_of(place.z * 128, 128), 128)
    loads = [
        pltpu.make_async_copy(src, dst, local_sems.at[i])
        for i, (src, dst) in enumerate(
            (
                (policy_hidden_hbm, policy_turned),
                (key_rows_hbm.at[:, kv_lanes], key_pair),
                (value_rows_hbm.at[:, kv_lanes], value_pair),
                (queries_hbm, queries),
                (out_weight_hbm, out_weight),
                (residual_hbm, residual_turned),
                (policy_head_hbm, policy_head),
                (ref_head_hbm, ref_head),
            )
        )
    ]
    l_policy, l_key, l_value, l_query, l_out, l_residual, l_policy_head, l_ref_head = loads
    for load in loads:
        load.start()

    barrier = pltpu.get_barrier_semaphore()
    ctx_count = lax.axis_size("ctx")
    next_ctx = lax.rem(place.ctx + 1, ctx_count)
    last_ctx = lax.rem(place.ctx + ctx_count - 1, ctx_count)
    for other in (next_ctx, last_ctx):
        pl.semaphore_signal(barrier, inc=1, device_id=(other, me), device_id_type=MESH)

    def greet(t, carry):
        pl.semaphore_signal(
            barrier,
            inc=1,
            device_id=(place.ctx, lax.rem(me + t, GROUP)),
            device_id_type=MESH,
        )
        return carry

    lax.fori_loop(1, GROUP, greet, 0)

    own_rows = pl.ds(pl.multiple_of(own * piece, piece), piece)

    def turn_over(source, out, land):
        for h in range(HALVES):
            out[h] = source[:, h * half_rows : (h + 1) * half_rows].T
        land[me] = out[:, own_rows, :]

    l_policy.wait()
    turn_over(policy_turned, policy_hidden, land_policy)

    upper = lax.rem(me // 2, 2) == 1
    l_key.wait()
    l_value.wait()
    for pair, lane in ((key_pair, 0), (value_pair, HEAD_DIM)):
        kv[pl.ds(WINDOW, rows), lane : lane + HEAD_DIM] = jnp.where(
            upper, pair[:, HEAD_DIM:], pair[:, :HEAD_DIM]
        )

    pl.semaphore_wait(barrier, GROUP - 1 + 2)

    pool = Pool(send_sems, recv_sems)
    halo = pool.start(kv.at[pl.ds(rows, WINDOW)], kv.at[pl.ds(0, WINDOW)], (next_ctx, me))

    def spread(source, land, sems, t):
        to = lax.rem(me + t, GROUP)
        block = pl.ds(pl.multiple_of(place.block_of(to) * piece, piece), piece)
        return pltpu.make_async_remote_copy(
            src_ref=source.at[:, block, :],
            dst_ref=land.at[me],
            send_sem=sems.at[0, t - 1],
            recv_sem=sems.at[1, t - 1],
            device_id=(place.ctx, to),
            device_id_type=MESH,
        )

    def each_peer(act):
        def body(t, carry):
            act(t)
            return carry

        lax.fori_loop(1, GROUP, body, 0)

    each_peer(lambda t: spread(policy_hidden, land_policy, policy_sems, t).start())
    l_residual.wait()
    turn_over(residual_turned, residual, land_residual)
    each_peer(lambda t: spread(residual, land_residual, residual_sems, t).start())

    def attend(block):
        at = block * WINDOW
        keys = kv[at : at + 2 * WINDOW, :HEAD_DIM]
        values = kv[at : at + 2 * WINDOW, HEAD_DIM:]
        query = queries[at : at + WINDOW, :]
        heads = query.shape[1] // HEAD_DIM
        offsets = (
            lax.broadcasted_iota(jnp.int32, (WINDOW, 2 * WINDOW), 0)
            + WINDOW
            - lax.broadcasted_iota(jnp.int32, (WINDOW, 2 * WINDOW), 1)
        )
        where_at = column(positions[block : block + 1, :].astype(F32))
        where_at = jnp.concatenate([where_at, where_at], axis=1)
        allowed = (offsets >= 0) & (offsets < WINDOW) & (where_at >= offsets.astype(F32))
        mixed = []
        for h in range(heads):
            scores = (
                lax.dot_general(
                    query[:, h * HEAD_DIM : (h + 1) * HEAD_DIM],
                    keys,
                    NT,
                    preferred_element_type=F32,
                )
                * HEAD_DIM**-0.5
            )
            scores = jnp.where(allowed, scores, -jnp.inf)
            sink = sinks[h]
            peak = jnp.maximum(jnp.max(scores, axis=1, keepdims=True), sink)
            raised = jnp.exp(scores - peak)
            total = jnp.sum(raised, axis=1, keepdims=True) + jnp.exp(sink - peak)
            weights = (raised / total).astype(BF)
            mixed.append(jnp.dot(weights, values, preferred_element_type=F32).astype(BF))
        attended[at : at + WINDOW, :] = jnp.concatenate(mixed, axis=1)

    def project(half):
        rows_in = attended[half * half_rows : (half + 1) * half_rows, :]
        for start in range(0, width, 512):
            stop = min(start + 512, width)
            partial_rows[half, :, :, start:stop] = (
                lax.dot_general(
                    rows_in, out_weight[start:stop, :], NT, preferred_element_type=F32
                )
                .astype(BF)
                .reshape(GROUP, piece, stop - start)
            )

    policy_ag = [Gather(pool, place, policy_rows.at[h], h) for h in range(HALVES)]
    normed_ag = [Gather(pool, place, normed_rows.at[h], h) for h in range(HALVES)]

    def scatter(x, bufs, h):
        return Scatter(pool, place, x.at[h], *(buf.at[h] for buf in bufs))

    p_bufs = (p_tp, p_tm, p_fp, p_fm, p_y, p_fa)
    g_bufs = (g_tp, g_tm, g_fp, g_fm, g_y, g_fa)
    partial_rs = [scatter(partial_rows, p_bufs, h) for h in range(HALVES)]
    grad_rs = [scatter(grad_parts, g_bufs, h) for h in range(HALVES)]

    def join(land, h):
        return jnp.concatenate([land[v, h] for v in range(GROUP)], axis=1)

    def normalise(h):
        projected = partial_rs[h].result() + bias[...].reshape(1, width)
        hidden = (residual_own[h].astype(F32) + projected).astype(BF)
        wide = hidden.astype(F32)
        spread_of = jnp.sum(wide * wide, axis=1, keepdims=True) * (1.0 / width)
        normed_rows[h, own] = (wide * lax.rsqrt(spread_of + 1e-05) * gain[...].reshape(1, width)).astype(BF)

    def logits(rows_of, head, out, h, tile, tiles=3):
        cols = slice(tile * (vocab_here // tiles), (tile + 1) * (vocab_here // tiles))
        lhs = rows_of[h].reshape(half_rows, width)
        out[h, :, cols] = jnp.dot(lhs, head[:, cols], preferred_element_type=F32)

    def policy_stats(h):
        top = jnp.max(policy_logits[h], axis=1, keepdims=True)
        pol_max[h] = jnp.broadcast_to(top, pol_max.shape[1:])
        pol_sum[h] = jnp.broadcast_to(
            jnp.sum(jnp.exp(policy_logits[h] - top), axis=1, keepdims=True), pol_sum.shape[1:]
        )

    def stat_copy(h, t):
        to = lax.rem(me + t, GROUP)
        return pltpu.make_async_remote_copy(
            src_ref=stats.at[h, me],
            dst_ref=stats.at[h, me],
            send_sem=stat_sems.at[h, 0, t - 1],
            recv_sem=stat_sems.at[h, 1, t - 1],
            device_id=(place.ctx, to),
            device_id_type=MESH,
        )

    def send_stats(h):
        top = jnp.max(ref_logits[h], axis=1, keepdims=True)
        total = jnp.sum(jnp.exp(ref_logits[h] - top), axis=1, keepdims=True)
        pol_top = pol_max[h][:, :1]
        gap = jnp.sum(
            jnp.exp(policy_logits[h] - pol_top) * (policy_logits[h] - ref_logits[h]),
            axis=1,
            keepdims=True,
        )
        lane = lax.broadcasted_iota(jnp.int32, (half_rows, 128), 1)
        packed = jnp.where(lane == 0, pol_max[h], pol_sum[h])
        packed = jnp.where(lane == 2, top, packed)
        packed = jnp.where(lane == 3, total, packed)
        packed = jnp.where(lane == 4, gap, packed)
        stats[h, me] = packed.T[:8, :]
        each_peer(lambda t: stat_copy(h, t).start())

    def loss_gradient(h):
        each_peer(lambda t: stat_copy(h, t).wait_recv())
        pol_tops, pol_sums = stats[h, :, 0, :], stats[h, :, 1, :]
        ref_tops, ref_sums = stats[h, :, 2, :], stats[h, :, 3, :]
        pol_top = jnp.max(pol_tops, axis=0, keepdims=True)
        ref_top = jnp.max(ref_tops, axis=0, keepdims=True)
        scale = jnp.exp(pol_tops - pol_top)
        pol_total = jnp.sum(pol_sums * scale, axis=0, keepdims=True)
        gap = jnp.sum(stats[h, :, 4, :] * scale, axis=0, keepdims=True) / pol_total
        ref_total = jnp.sum(ref_sums * jnp.exp(ref_tops - ref_top), axis=0, keepdims=True)
        log_pol = pol_top + jnp.log(pol_total)
        log_ref = ref_top + jnp.log(ref_total)
        divergence = gap - log_pol + log_ref
        for part in range(half_rows // 128):
            lanes = slice(part * 128, (part + 1) * 128)
            at = h * (half_rows // 128) + part
            here = slice(part * 128, (part + 1) * 128)
            divergence_out[at : at + 1, :] = divergence[:, lanes]
            adv_row = advantages[at : at + 1, :]
            log_col = column(log_pol[:, lanes])
            add_col = column(adv_row - gap[:, lanes])
            adv_col = column(adv_row)
            tok_col = column(
                (token_ids[at : at + 1, :] - me * vocab_here).astype(F32)
            )
            for chunk in range(0, vocab_here, 128):
                cols = slice(chunk, chunk + 128)
                ids = (lax.broadcasted_iota(jnp.int32, (128, 128), 1) + chunk).astype(F32)
                pol = policy_logits[h, here, cols]
                prob = jnp.exp(pol - log_col)
                value = prob * (pol - ref_logits[h, here, cols] + add_col)
                logit_grad[h, here, cols] = (
                    value - jnp.where(ids == tok_col, adv_col, 0.0)
                ).astype(BF)

    def gradient(h, db):
        at = pl.ds(SIDE * place.along_b(db), SIDE)
        block_rows = head_blocks.shape[1]
        lhs = head_blocks[at].reshape(SIDE * block_rows, vocab_here)
        grad_parts[h, at] = (
            lax.dot_general(lhs, logit_grad[h], NT, preferred_element_type=F32)
            .astype(BF)
            .reshape(SIDE, block_rows, half_rows)
        )

    def finish(h):
        grad_out[:, h * half_rows : (h + 1) * half_rows] = grad_rs[h].result()[:share, :]

    one, two = 1, 0
    l_query.wait()
    attend(2)
    attend(3)
    l_out.wait()
    project(one)
    partial_rs[one].far()
    l_policy_head.wait()
    for d in range(GROUP):
        head_blocks[place.block_of(d), :share, :] = policy_head[d * share : (d + 1) * share, :]
    halo.wait_recv()
    attend(1)
    partial_rs[one].near_down()
    partial_rs[one].near_up()
    attend(0)
    project(two)
    partial_rs[two].far()
    partial_rs[one].pass_up()
    partial_rs[one].pass_down()
    partial_rs[two].near_down()
    each_peer(lambda t: spread(policy_hidden, land_policy, policy_sems, t).wait_recv())
    policy_rows[one, own] = join(land_policy, one)
    policy_ag[one].s0()
    partial_rs[two].pass_down()
    partial_rs[two].near_up()
    partial_rs[two].pass_up()
    partial_rs[one].turn()
    each_peer(lambda t: spread(residual, land_residual, residual_sems, t).wait_recv())
    residual_own[two] = join(land_residual, two)
    policy_ag[one].s4()
    policy_rows[two, own] = join(land_policy, two)
    residual_own[one] = join(land_residual, one)
    policy_ag[one].s1()
    policy_ag[one].s2()
    partial_rs[two].turn()
    normalise(one)
    normed_ag[one].s0()
    policy_ag[one].s3()
    policy_ag[two].s0()
    normed_ag[one].s2()
    normalise(two)
    normed_ag[two].s0()
    policy_ag[two].s2()
    policy_ag[two].s1()
    policy_ag[one].s7()
    normed_ag[one].s3()
    normed_ag[one].s1()
    policy_ag[one].s5()
    normed_ag[one].s4()
    policy_ag[one].s6()
    normed_ag[one].s6()
    normed_ag[two].s1()
    normed_ag[one].s5()
    policy_ag[two].s3()
    policy_ag[two].s5()
    policy_ag[two].s4()
    normed_ag[two].s4()
    normed_ag[one].s7()
    normed_ag[two].s2()
    policy_ag[two].s6()
    policy_ag[one].s8()
    logits(policy_rows, policy_head, policy_logits, one, 0)
    logits(policy_rows, policy_head, policy_logits, one, 1)
    normed_ag[two].s3()
    logits(policy_rows, policy_head, policy_logits, one, 2)
    policy_ag[two].s7()
    policy_stats(one)
    normed_ag[two].s5()
    normed_ag[one].s8()
    l_ref_head.wait()
    logits(normed_rows, ref_head, ref_logits, one, 0)
    normed_ag[two].s6()
    logits(normed_rows, ref_head, ref_logits, one, 1)
    logits(normed_rows, ref_head, ref_logits, one, 2)
    normed_ag[two].s7()
    send_stats(one)
    policy_ag[two].s8()
    logits(policy_rows, policy_head, policy_logits, two, 0)
    logits(policy_rows, policy_head, policy_logits, two, 1)
    logits(policy_rows, policy_head, policy_logits, two, 2)
    normed_ag[two].s8()
    policy_stats(two)
    logits(normed_rows, ref_head, ref_logits, two, 0)
    logits(normed_rows, ref_head, ref_logits, two, 1)
    logits(normed_rows, ref_head, ref_logits, two, 2)
    send_stats(two)
    loss_gradient(one)
    gradient(one, 2)
    grad_rs[one].far()
    gradient(one, 1)
    gradient(one, -1)
    grad_rs[one].near_up()
    gradient(one, 0)
    grad_rs[one].near_down()
    grad_rs[one].pass_up()
    grad_rs[one].pass_down()
    loss_gradient(two)
    gradient(two, 2)
    grad_rs[two].far()
    gradient(two, 1)
    gradient(two, -1)
    grad_rs[two].near_up()
    grad_rs[two].near_down()
    grad_rs[two].pass_down()
    grad_rs[two].pass_up()
    grad_rs[one].turn()
    gradient(two, 0)
    grad_rs[two].turn()
    finish(one)
    finish(two)

    for copy in pool.copies:
        copy.wait_send()
    each_peer(lambda t: spread(policy_hidden, land_policy, policy_sems, t).wait_send())
    each_peer(lambda t: spread(residual, land_residual, residual_sems, t).wait_send())
    for h in range(HALVES):
        each_peer(lambda t: stat_copy(h, t).wait_send())


def hand_over(divergence, grad, divergence_out, grad_out):
    divergence_out[...] = divergence[...]
    grad_out[...] = grad[...]


def shards(
    queries,
    key_rows,
    value_rows,
    sink_logits,
    out_weight,
    out_bias,
    residual,
    norm_gain,
    policy_hidden,
    ref_head,
    policy_head,
    token_ids,
    advantages,
    positions,
):
    rows, heads_width = queries.shape
    share = residual.shape[1]
    width, vocab_here = ref_head.shape
    half_rows = rows // HALVES
    piece = half_rows // GROUP
    block_rows = -(-share // 16) * 16
    copies = 1 + HALVES * 2 * (15 + 9)

    def sums(block):
        return [
            pltpu.VMEM((HALVES, lead, *block), BF)
            for lead in (2, 2, SIDE, SIDE, SIDE - 1, SIDE - 1)
        ]

    vmem, hbm = (pl.BlockSpec(memory_space=space) for space in (pltpu.VMEM, pl.ANY))
    smem = pl.BlockSpec(memory_space=pltpu.SMEM)
    divergence, grad = pl.pallas_call(
        kernel,
        out_shape=(
            jax.ShapeDtypeStruct((rows // 128, 128), F32),
            jax.ShapeDtypeStruct((share, rows), F32),
        ),
        in_specs=[
            hbm, hbm, hbm, smem, hbm, vmem, hbm, vmem, hbm, hbm, hbm, vmem, vmem, vmem,
        ],
        out_specs=(vmem, vmem),
        scratch_shapes=[
            pltpu.VMEM((width, heads_width), BF),
            pltpu.VMEM((width, vocab_here), BF),
            pltpu.VMEM((width, vocab_here), BF),
            pltpu.VMEM((GROUP, block_rows, vocab_here), BF),
            pltpu.VMEM((rows, heads_width), BF),
            pltpu.VMEM((rows, 2 * HEAD_DIM), BF),
            pltpu.VMEM((rows, 2 * HEAD_DIM), BF),
            pltpu.VMEM((share, rows), BF),
            pltpu.VMEM((share, rows), BF),
            pltpu.VMEM((HALVES, half_rows, share), BF),
            pltpu.VMEM((HALVES, half_rows, share), BF),
            pltpu.VMEM((WINDOW + rows, 2 * HEAD_DIM), BF),
            pltpu.VMEM((rows, heads_width), BF),
            pltpu.VMEM((GROUP, HALVES, piece, share), BF),
            pltpu.VMEM((GROUP, HALVES, piece, share), BF),
            pltpu.VMEM((HALVES, piece, width), BF),
            pltpu.VMEM((HALVES, GROUP, piece, width), BF),
            pltpu.VMEM((HALVES, GROUP, piece, width), BF),
            pltpu.VMEM((HALVES, GROUP, piece, width), BF),
            pltpu.VMEM((HALVES, half_rows, vocab_here), F32),
            pltpu.VMEM((HALVES, half_rows, vocab_here), F32),
            pltpu.VMEM((HALVES, half_rows, vocab_here), BF),
            pltpu.VMEM((HALVES, GROUP, block_rows, half_rows), BF),
            pltpu.VMEM((HALVES, half_rows, 128), F32),
            pltpu.VMEM((HALVES, half_rows, 128), F32),
            pltpu.VMEM((HALVES, GROUP, 8, half_rows), F32),
            *sums((piece, width)),
            *sums((block_rows, half_rows)),
            pltpu.SemaphoreType.DMA((8,)),
            pltpu.SemaphoreType.DMA((copies,)),
            pltpu.SemaphoreType.DMA((copies,)),
            pltpu.SemaphoreType.DMA((2, GROUP - 1)),
            pltpu.SemaphoreType.DMA((2, GROUP - 1)),
            pltpu.SemaphoreType.DMA((HALVES, 2, GROUP - 1)),
        ],
        compiler_params=pltpu.CompilerParams(
            collective_id=0, has_side_effects=True, vmem_limit_bytes=62 << 20
        ),
    )(
        queries,
        key_rows,
        value_rows,
        sink_logits,
        out_weight.T,
        out_bias,
        residual.T,
        norm_gain,
        policy_hidden.T,
        ref_head,
        policy_head,
        token_ids.reshape(rows // 128, 128),
        advantages.reshape(rows // 128, 128),
        positions.reshape(rows // 128, 128),
    )
    divergence, grad = pl.pallas_call(
        hand_over,
        out_shape=(
            jax.ShapeDtypeStruct(divergence.shape, F32),
            jax.ShapeDtypeStruct(grad.shape, F32),
        ),
        in_specs=[vmem, vmem],
        out_specs=(vmem, vmem),
    )(divergence, grad)
    return divergence.reshape(rows), grad


def solution(mesh):
    return jax.shard_map(
        shards,
        mesh=mesh,
        in_specs=(
            P("ctx", "vocab"),
            P("ctx", None),
            P("ctx", None),
            P("vocab"),
            P("vocab", None),
            P(),
            P("ctx", "vocab"),
            P(),
            P("ctx", "vocab"),
            P(None, "vocab"),
            P(None, "vocab"),
            P("ctx"),
            P("ctx"),
            P("ctx"),
        ),
        out_specs=(P("ctx"), P("vocab", "ctx")),
        check_vma=False,
    )
```
